128 devices in a mesh: doc: 8 (over z, core), feat: 16 (over x, y).
Axes of the slice: x: 4, y: 4, z: 4, core: 2. Of those that a mesh axis runs over, the one named last changes fastest.
Arguments:
- documents: bfloat16 [1024, 512], P('doc', 'feat'), may hold values from -6 to 6
- directions: bfloat16 [512, 32768], P('doc', 'feat'), may hold values from -0.5 to 0.5
- phase: float32 [32768], P('feat'), may hold values from -3.140625 to 3.140625
- amplitude: float32 [32768], P('feat'), may hold values from 0.4 to 2.3
- doc_weight: float32 [1024], P('doc'), may hold values from 0.5 to 4.2
- labels: int32 [1024], P('doc'), may hold values from 0 to 127
Outputs:
- margins: float32 [1024, 128], P('doc')
- scaled_weights: float32 [32768, 128], P('feat')
The draws below stay inside these ranges and needn't reach their ends.
All inputs are finite; a program needn't handle non-finite values.
Results may differ from the reference program's by a relative error of at most 0.0003.
Values may be sent and summed in bfloat16 or wider, within the bound.
No kernel may reach another device: no remote copies, remote signals or barrier semaphores. Data moves between devices by JAX's collectives and lax.ppermute only.
A program may use at most 64 MiB of HBM per device.

```python
import jax
import jax.numpy as jnp
from jax import lax

F = 512
W = 32768
C = 128
DOC_DEV = 128
ITERS = 3
NEWTON = 3
NDOC = 1024
N_DOC = 8
N_FEAT = 16


def draw_amplitude(key, part):
    ramp = 0.6 + 1.2 * jnp.arange(W, dtype=jnp.float32) / (W - 1)
    spread = jax.random.uniform(key, (W,), jnp.float32, 0.8, 1.2)
    return ramp * spread


def draw_doc_weight(key, part):
    ramp = 1.0 + 2.0 * jnp.arange(NDOC, dtype=jnp.float32) / (NDOC - 1)
    spread = jax.random.uniform(key, (NDOC,), jnp.float32, 0.7, 1.3)
    return ramp * spread


def with_ends(entries, own_key, smallest, high):
    longest = entries.shape.index(max(entries.shape))
    spots = []
    for shift in (0, 1):
        where = [jax.random.randint(jax.random.fold_in(own_key, axis), (), 0, length) for axis, length in enumerate(entries.shape)]
        where[longest] = (where[longest] + shift) % entries.shape[longest]
        spots.append(tuple(where))
    return entries.at[spots[0]].set(smallest).at[spots[1]].set(high)


def block_scale(key, extent, shards, smallest, largest):
    def one(position, parts):
        heights = jax.random.uniform(jax.random.fold_in(jax.random.fold_in(key, 6), position), (parts,), jnp.float32, smallest / len(shards), largest / len(shards))
        return jnp.repeat(jnp.exp(heights), extent[position] // parts).reshape((-1,) + (1,) * (len(extent) - position - 1))

    level = one(*shards[0])
    for cut in shards[1:]:
        level = level * one(*cut)
    return level


def normal_values(stream_key, shape, width, most, shards=(), held_as=jnp.bfloat16):
    values = width * jax.random.normal(stream_key, shape, jnp.float32)
    if shards:
        values = values * block_scale(stream_key, shape, shards, -0.22, 0.18)
    return jnp.clip(values, -most, most).astype(held_as)


def setup_inputs(seed: int = 0) -> dict:
    keys = jax.random.split(jax.random.key(seed), 7)
    documents = normal_values(keys[0], (NDOC, F), 1.0, 6.0, ((0, 8), (1, 16)))
    directions = normal_values(keys[1], (F, W), (F // 4) ** -0.5, 0.5, ((0, 8), (1, 16)))
    phase = jnp.clip(jax.random.uniform(keys[2], (W,), jnp.float32, -3.140625, 3.140625), -3.140625, 3.140625)
    amplitude = draw_amplitude(jax.random.fold_in(keys[6], 71), 0)
    doc_weight = draw_doc_weight(jax.random.fold_in(keys[6], 71), 0)
    labels = with_ends(jax.random.randint(keys[5], (NDOC,), 0, C), jax.random.fold_in(keys[5], 1), 0, C - 1).astype(jnp.int32)
    return dict(documents=documents, directions=directions, phase=phase, amplitude=amplitude, doc_weight=doc_weight, labels=labels)


shrink_level = 0.1
ratio_floor = 1e-06

def feature_tile(documents, directions, phase, amplitude, row_block, col_block):
    width_tile = W // N_FEAT
    doc_rows = lax.dynamic_slice_in_dim(documents, (row_block * DOC_DEV).astype(jnp.int32), DOC_DEV, 0)
    dir_cols = lax.dynamic_slice_in_dim(directions, (col_block * width_tile).astype(jnp.int32), width_tile, 1)
    phase_cols = lax.dynamic_slice_in_dim(phase, (col_block * width_tile).astype(jnp.int32), width_tile, 0)
    amp_cols = lax.dynamic_slice_in_dim(amplitude, (col_block * width_tile).astype(jnp.int32), width_tile, 0)
    angles = jnp.dot(doc_rows.astype(jnp.float32), dir_cols.astype(jnp.float32), preferred_element_type=jnp.float32)
    return jnp.sqrt(2.0 / width_tile) * amp_cols * jnp.cos(angles + phase_cols)

def project_tile(features, factor, start, target):
    residue = target - jnp.dot(features, start, precision=lax.Precision.HIGHEST)
    halfway = lax.linalg.triangular_solve(factor, residue, left_side=True, lower=True)
    solved = lax.linalg.triangular_solve(factor, halfway, left_side=True, lower=True, transpose_a=True)
    new_copy = start + lax.dot_general(features, solved, (((0,), (0,)), ((), ())), precision=lax.Precision.HIGHEST)
    new_part = jnp.dot(features, new_copy, precision=lax.Precision.HIGHEST)
    return (new_copy, new_part)

def logistic_prox(target, signs, weight_ratio):
    current = target
    for newton_step in range(NEWTON):
        chance = jax.nn.sigmoid(-signs * current)
        gradient = current - target - weight_ratio * signs * chance
        current = current - gradient / (1.0 + weight_ratio * chance * (1.0 - chance))
    return current

def shrink_values(target, limit):
    return target - jnp.clip(target, -limit, limit)

def reference(documents, directions, phase, amplitude, doc_weight, labels):
    width_tile = W // N_FEAT
    tile_count = N_DOC * N_FEAT
    tile_index = jnp.arange(tile_count, dtype=jnp.int32)

    def factor_tile(tile):
        features = feature_tile(documents, directions, phase, amplitude, tile // N_FEAT, tile % N_FEAT)
        gram = jnp.eye(DOC_DEV, dtype=jnp.float32) + lax.dot_general(features, features, (((1,), (1,)), ((), ())), precision=lax.Precision.HIGHEST)
        return jnp.linalg.cholesky(gram)
    factors = lax.map(factor_tile, tile_index)
    signs = jnp.where(labels[:, None] == jnp.arange(C, dtype=jnp.int32)[None, :], 1.0, -1.0).astype(jnp.float32)
    loss_weight = doc_weight[:, None]
    rho = jnp.float32(1.0)
    margins = logistic_prox(jnp.zeros((NDOC, C), jnp.float32), signs, loss_weight / rho)
    sums = jnp.zeros((NDOC, C), jnp.float32)
    duals_y = jnp.zeros((NDOC, C), jnp.float32)
    duals_x = jnp.zeros((N_DOC, N_FEAT, width_tile, C), jnp.float32)
    partial_value = jnp.zeros((N_DOC, N_FEAT, DOC_DEV, C), jnp.float32)
    weights = jnp.zeros((N_FEAT, width_tile, C), jnp.float32)
    for step in range(ITERS):
        fix_blocks = ((margins - duals_y - sums) / N_FEAT).reshape(N_DOC, DOC_DEV, C)

        def tile_step(tile):
            row_block = tile // N_FEAT
            col_block = tile % N_FEAT
            features = feature_tile(documents, directions, phase, amplitude, row_block, col_block)
            start = weights[col_block] - duals_x[row_block, col_block]
            target = partial_value[row_block, col_block] + fix_blocks[row_block]
            return project_tile(features, factors[tile], start, target)
        new_copy, new_part = lax.map(tile_step, tile_index)
        new_copy = new_copy.reshape(N_DOC, N_FEAT, width_tile, C)
        partial_value = new_part.reshape(N_DOC, N_FEAT, DOC_DEV, C)
        sums = lax.optimization_barrier(jnp.sum(partial_value, axis=1)).reshape(NDOC, C)
        old_weights = weights
        old_margins = margins
        weights = shrink_values(lax.optimization_barrier(jnp.sum(new_copy + duals_x, axis=0)) / N_DOC, shrink_level / (rho * N_DOC))
        margins = logistic_prox(sums + duals_y, signs, loss_weight / rho)
        duals_x = duals_x + new_copy - weights[None]
        duals_y = duals_y + sums - margins
        if step + 1 < ITERS:
            primal = jnp.sum((new_copy - weights[None]) ** 2) + jnp.sum((sums - margins) ** 2)
            dual_norm = rho * rho * (N_DOC * jnp.sum((weights - old_weights) ** 2) + jnp.sum((margins - old_margins) ** 2))
            growth = ((primal + ratio_floor) / (dual_norm + ratio_floor)) ** 0.25
            rho = rho * growth
            duals_x = duals_x / growth
            duals_y = duals_y / growth
    return (margins, N_FEAT * weights.reshape(W, C))
```

```python
import functools

import jax
import jax.numpy as jnp
from jax import lax
from jax.experimental import pallas as pl
from jax.experimental.pallas import tpu as pltpu
from jax.sharding import PartitionSpec as P

C = 128
ITERS = 3
NEWTON = 3
ND = 8
NF = 16
ROWS = 128
CHUNK = 256

shrink_level = 0.1
ratio_floor = 1e-06

AXES = ("doc", "feat")
F32 = jnp.float32
BF16 = jnp.bfloat16
VMEM_LIMIT = 50 * 1024 * 1024
SIN_TERMS = (
    -2.388494735328095e-08,
    2.752503405645257e-06,
    -0.00019840856839437038,
    0.008333330973982811,
    -0.1666666716337204,
    1.0,
)
INV_TWO_PI = 0.15915494309189535
PI_HIGH = 3.140625
PI_LOW = 0.0009676535897932


def nn(a, b):
    return lax.dot_general(a, b, (((1,), (0,)), ((), ())), preferred_element_type=F32)


def nt(a, b):
    return lax.dot_general(a, b, (((1,), (1,)), ((), ())), preferred_element_type=F32)


def tn(a, b):
    return lax.dot_general(a, b, (((0,), (0,)), ((), ())), preferred_element_type=F32)


def split(v):
    high = v.astype(BF16)
    return high, (v - high.astype(F32)).astype(BF16)


def product(a, b, dot=nn):
    ah, al = split(a)
    bh, bl = split(b)
    return dot(ah, bh) + (dot(ah, bl) + dot(al, bh))


def scaled_cos(angle, scale):
    turns = jnp.round(angle * INV_TWO_PI)
    half = (angle * 0.5 - turns * PI_HIGH) - turns * PI_LOW
    square = half * half
    series = SIN_TERMS[0]
    for term in SIN_TERMS[1:]:
        series = series * square + term
    sine = series * half
    return scale - (scale + scale) * (sine * sine)


def logistic_prox(target, signs, weight_ratio):
    current = target
    for _ in range(NEWTON):
        chance = 1.0 / (1.0 + jnp.exp(signs * current))
        gradient = current - target - weight_ratio * signs * chance
        current = current - gradient / (1.0 + weight_ratio * chance * (1.0 - chance))
    return current


def signs_of(labels_ref):
    labels = labels_ref[...]
    classes = lax.broadcasted_iota(jnp.int32, (C, ROWS), 0)
    return jnp.where(jnp.broadcast_to(labels, (C, ROWS)) == classes, 1.0, -1.0).astype(F32)


def total(v):
    return jnp.sum(jnp.sum(v, axis=0, keepdims=True), axis=1, keepdims=True)


def pack(values):
    lane = lax.broadcasted_iota(jnp.int32, (8, 128), 1)
    out = jnp.zeros((8, 128), F32)
    for k, v in enumerate(values):
        if v is not None:
            out = jnp.where(lane == k, jnp.broadcast_to(v, (8, 128)), out)
    return out


def inverse(matrix):
    n = matrix.shape[0]
    row_id = lax.broadcasted_iota(jnp.int32, (n, n), 0)
    col_id = lax.broadcasted_iota(jnp.int32, (n, n), 1)
    lane = lax.broadcasted_iota(jnp.int32, (1, n), 1)
    sub = lax.broadcasted_iota(jnp.int32, (n, 1), 0)
    m = matrix
    for k in range(n):
        recip = 1.0 / m[k : k + 1, k : k + 1]
        row = jnp.where(lane == k, recip, m[k : k + 1, :] * recip)
        col = jnp.where(sub == k, -1.0, m[:, k : k + 1])
        m = jnp.where((row_id == k) | (col_id == k), 0.0, m) - col * row
    return m


def doc_piece(docs_ref, slot):
    z = lax.axis_index("doc") // 2
    core = lax.axis_index("doc") % 2
    block = ((z - slot // 2 + 4) % 4) * 2 + (core + slot % 2) % 2
    rows = ROWS // 2
    return docs_ref[pl.ds(pl.multiple_of(rows * block, rows), rows), :]


def own_kernel(docs, phase, amp, labels, weight, d0, d1, d2, d3, e0, e1, e2, e3,
               high, low, inv_ref, prox_ref, send):
    dirs = (d0, e0, d1, e1, d2, e2, d3, e3)
    left = jnp.concatenate([doc_piece(docs, s) for s in range(ND)], axis=0)
    width = phase.shape[1]
    amp_scale = (2.0 / width) ** 0.5
    gram = jnp.zeros((ROWS, 2 * ROWS), F32)
    for start in range(0, width, CHUNK):
        cols = pl.ds(start, CHUNK)
        right = jnp.concatenate([d[:, cols] for d in dirs], axis=0)
        angle = tn(left, right) + phase[:, cols]
        value = scaled_cos(angle, amp[:, cols] * amp_scale)
        vh, vl = split(value)
        high[:, cols] = vh
        low[:, cols] = vl
        gram = gram + nt(vh, jnp.concatenate([vh, vl], axis=0))
    cross = gram[:, ROWS:]
    row_id = lax.broadcasted_iota(jnp.int32, (ROWS, ROWS), 0)
    col_id = lax.broadcasted_iota(jnp.int32, (ROWS, ROWS), 1)
    whole = gram[:, :ROWS] + (cross + cross.T) + jnp.where(row_id == col_id, 1.0, 0.0)
    inv = inverse(whole)
    inv_ref[...] = inv
    signs = signs_of(labels)
    margins = logistic_prox(jnp.zeros((C, ROWS), F32), signs, weight[...])
    prox_ref[...] = margins
    right_side = margins * (1.0 / NF)
    w = product(right_side, inv)
    send[0:C, :] = w
    send[C : C + 8, :] = pack([None, None, total(w * (right_side - w))])


def other_kernel(docs, docs_o, phase, amp, d0, d1, d2, d3, e0, e1, e2, e3, *refs):
    high, low, left_ref = refs
    dirs = (d0, e0, d1, e1, d2, e2, d3, e3)
    width = phase.shape[1]
    amp_scale = (2.0 / width) ** 0.5
    for s in range(ND):
        left_ref[s * 64 : s * 64 + 64, :] = jnp.concatenate(
            [doc_piece(docs_o.at[b], s) for b in range(ND - 1)], axis=1
        )

    def step(c, carry):
        cols = pl.ds(pl.multiple_of(c * CHUNK, CHUNK), CHUNK)
        right = jnp.concatenate([d[:, cols] for d in dirs], axis=0)
        scale = amp[:, cols] * amp_scale
        turn = phase[:, cols]
        for b in range(ND - 1):
            angle = tn(left_ref[:, b * ROWS : (b + 1) * ROWS], right) + turn
            vh, vl = split(scaled_cos(angle, scale))
            high[b * ROWS : (b + 1) * ROWS, cols] = vh
            low[b * ROWS : (b + 1) * ROWS, cols] = vl
        return carry

    lax.fori_loop(0, width // CHUNK, step, 0)


def step_kernel(k, last, *refs):
    it = iter(refs)
    take = lambda n: [next(it) for _ in range(n)]
    feat_in = take(4)
    own = next(it)
    zs, = take(1)
    cores, = take(1)
    oh, ol, th, tl, inv_ref, labels, weight = take(7)
    if k == 1:
        prox_prev, = take(1)
    else:
        z_prev, v_prev, e_prev, small = take(4)
    if last:
        out_m, out_z = take(2)
    else:
        z_out, v_out, e_out, small_out, send = take(5)
    gather_h, gather_l = take(2)
    width = oh.shape[1]
    n_rows = own.shape[0]

    def feat_total(rows):
        return (feat_in[0][rows, :] + feat_in[1][rows, :]) + (feat_in[2][rows, :] + feat_in[3][rows, :])

    def doc_block(slot, rows):
        if slot == 0:
            return own[rows, :]
        far, other = slot // 2, slot % 2
        ref = cores.at[far] if other else zs.at[far - 1]
        return ref[rows, :]

    tail = pl.ds(n_rows - 8, 8)
    feat_scalars = feat_total(tail)[0:1, :]
    doc_scalars = doc_block(0, tail)[0:1, :]
    for slot in range(1, ND):
        doc_scalars = doc_scalars + doc_block(slot, tail)[0:1, :]
    first = pl.ds(0, C)
    second = pl.ds(C, C)
    at = lambda row, n: row[:, n : n + 1]
    if k == 1:
        rho = jnp.ones((1, 1), F32)
        inv_g = None
        quad = at(doc_scalars, 2)
    else:
        rho_prev = small[7 * C : 7 * C + 1, 0:1]
        primal = at(feat_scalars, 0) + at(doc_scalars, 5)
        dual = rho_prev * rho_prev * (ND * at(feat_scalars, 1) + at(doc_scalars, 6))
        g = jnp.sqrt(jnp.sqrt((primal + ratio_floor) / (dual + ratio_floor)))
        rho = rho_prev * g
        inv_g = 1.0 / g
        quad = at(doc_scalars, 2) + inv_g * (at(doc_scalars, 3) + inv_g * at(doc_scalars, 4))

    own_q = None
    for slot in range(ND):
        q = doc_block(slot, first)
        if k > 1:
            q = q + doc_block(slot, second) * inv_g
        if slot == 0:
            own_q = q
        qh, ql = split(q)
        gather_h[:, slot * ROWS : (slot + 1) * ROWS] = qh
        gather_l[:, slot * ROWS : (slot + 1) * ROWS] = ql

    limit = shrink_level / (rho * ND)
    qh_own = gather_h[:, 0:ROWS]
    ql_own = gather_l[:, 0:ROWS]
    q_own2 = jnp.concatenate([qh_own, ql_own], axis=0)
    qh_rest = gather_h[:, ROWS:]
    q_rest2 = jnp.concatenate([qh_rest, gather_l[:, ROWS:]], axis=0)

    def chunk(c, carry):
        az, norm_p, norm_d = carry
        cols = pl.ds(pl.multiple_of(c * CHUNK, CHUNK), CHUNK)
        ah = oh[:, cols]
        al = ol[:, cols]
        both = nn(q_rest2, th[:, cols]) + nn(q_own2, ah)
        cross = nn(qh_rest, tl[:, cols]) + nn(qh_own, al)
        qsum = both[:C] + (both[C:] + cross)
        if k == 1:
            v = qsum
            target = v * (1.0 / ND)
            z = target - jnp.clip(target, -limit, limit)
            e = -z
            p = e
        else:
            v = qsum + v_prev[:, cols] * inv_g
            z_old = z_prev[:, cols]
            target = z_old + v * (1.0 / ND)
            z = target - jnp.clip(target, -limit, limit)
            e = z_old - z
            p = e - e_prev[:, cols] * inv_g
        if last:
            out_z[cols, :] = (z * float(NF)).T
            return carry
        v_out[:, cols] = v
        z_out[:, cols] = z
        e_out[:, cols] = e
        norm_p = norm_p + jnp.sum(p * (ND * p + 2.0 * qsum), axis=0, keepdims=True)
        norm_d = norm_d + jnp.sum(e * e, axis=0, keepdims=True)
        zh, zl = split(z)
        az2 = nt(jnp.concatenate([zh, zl], axis=0), ah)
        az = az + ((az2[:C] + az2[C:]) + nt(zh, al))
        return az, norm_p, norm_d

    init = (jnp.zeros((C, ROWS), F32), jnp.zeros((1, CHUNK), F32), jnp.zeros((1, CHUNK), F32))
    az, norm_p, norm_d = lax.fori_loop(0, width // CHUNK, chunk, init)

    signs = signs_of(labels)
    ratio = weight[...] / rho
    w_sum = feat_total(first)
    if k == 1:
        m_prev = prox_prev[...]
    else:
        m_prev = small[0:C, :]
        w_sum = w_sum + (feat_total(second) + small[C : 2 * C, :]) * inv_g
    target = m_prev - w_sum
    margins = logistic_prox(target, signs, ratio)
    if last:
        out_m[...] = margins.T
        return
    if k == 1:
        b_prev = jnp.zeros((C, ROWS), F32)
        w = own_q
        y = m_prev * (1.0 / NF) - w
        az_prev = jnp.zeros((C, ROWS), F32)
    else:
        b_prev = small[2 * C : 3 * C, :] * inv_g
        w = own_q + small[3 * C : 4 * C, :] * inv_g
        y = small[4 * C : 5 * C, :] + (m_prev - b_prev - small[5 * C : 6 * C, :]) * (1.0 / NF) - w
        az_prev = small[6 * C : 7 * C, :]
    b_new = target - margins
    sums = target - b_prev
    small_out[0:C, :] = margins
    small_out[C : 2 * C, :] = w_sum
    small_out[2 * C : 3 * C, :] = b_new
    small_out[3 * C : 4 * C, :] = w
    small_out[4 * C : 5 * C, :] = y
    small_out[5 * C : 6 * C, :] = sums
    small_out[6 * C : 7 * C, :] = az
    small_out[7 * C : 7 * C + 8, :] = jnp.broadcast_to(rho, (8, 128))
    ru = y + (margins - sums) * (1.0 / NF) - az
    rv = az_prev - az - w - b_new * (1.0 / NF)
    solved = product(jnp.concatenate([ru, rv], axis=0), inv_ref[...])
    u = solved[:C]
    v2 = solved[C:]
    send[0:C, :] = u
    send[C : 2 * C, :] = v2
    part = rv - v2
    gap = sums - margins
    move = margins - m_prev
    send[2 * C : 2 * C + 8, :] = pack(
        [
            jnp.sum(norm_p, axis=1, keepdims=True) + quad,
            jnp.sum(norm_d, axis=1, keepdims=True),
            total(u * (ru - u)),
            2.0 * total(u * part),
            total(v2 * part),
            total(gap * gap),
            total(move * move),
        ]
    )


def table(move):
    pairs = []
    for d in range(ND):
        for f in range(NF):
            z, core, x, y = d // 2, d % 2, f // 4, f % 4
            z2, core2, x2, y2 = move(z, core, x, y)
            pairs.append((d * NF + f, ((z2 % 4) * 2 + core2) * NF + (x2 % 4) * 4 + y2 % 4))
    return pairs


def along_y(v, k):
    return lax.ppermute(v, AXES, table(lambda z, c, x, y: (z, c, x, y + k)))


def along_x(v, k):
    return lax.ppermute(v, AXES, table(lambda z, c, x, y: (z, c, x + k, y)))


def along_z(v, k):
    return lax.ppermute(v, AXES, table(lambda z, c, x, y: (z + k, c, x, y)))


def across(v):
    return lax.ppermute(v, AXES, table(lambda z, c, x, y: (z, 1 - c, x, y)))


def call(body, outs, scratch=()):
    return pl.pallas_call(
        body,
        out_shape=outs,
        scratch_shapes=list(scratch),
        compiler_params=pltpu.CompilerParams(vmem_limit_bytes=VMEM_LIMIT),
    )


def shape(*dims, dtype=F32):
    return jax.ShapeDtypeStruct(dims, dtype)


def exchange(send):
    zs = [along_z(send, k) for k in (1, 2, 3)]
    ys = [along_y(send, k) for k in (1, 2, 3)]
    line = (send + ys[0]) + (ys[1] + ys[2])
    xs = [along_x(line, k) for k in (1, 2, 3)]
    zs = jnp.stack(zs)
    cores = across(jnp.concatenate([send[None], zs], axis=0))
    return [line] + xs + [send, zs, cores]


def per_device(documents, directions, phase, amplitude, doc_weight, labels):
    width = directions.shape[1]
    dirs = [directions] + [along_z(directions, k) for k in (1, 2, 3)]
    dirs_other = [across(d) for d in dirs]
    docs_t = documents.T
    docs = lax.all_to_all(
        jnp.broadcast_to(docs_t[None], (NF,) + docs_t.shape), "feat", 0, 0
    ).reshape(-1, ROWS)
    phase = phase.reshape(1, width)
    amp = amplitude.reshape(1, width)
    labels = labels.reshape(1, ROWS)
    weight = doc_weight.reshape(1, ROWS)
    all_dirs = dirs + dirs_other
    high, low, inv, prox, send = call(
        own_kernel,
        [
            shape(ROWS, width, dtype=BF16),
            shape(ROWS, width, dtype=BF16),
            shape(ROWS, ROWS),
            shape(C, ROWS),
            shape(C + 8, ROWS),
        ],
    )(docs, phase, amp, labels, weight, *all_dirs)

    docs_z = [along_z(docs, k) for k in (1, 2, 3)]
    docs_c = across(jnp.stack([docs] + docs_z))
    docs_o = jnp.stack(
        [docs_c[0], docs_z[0], docs_c[1], docs_z[1], docs_c[2], docs_z[2], docs_c[3]]
    )
    others = (ND - 1) * ROWS
    far_high, far_low = call(
        other_kernel,
        [shape(others, width, dtype=BF16), shape(others, width, dtype=BF16)],
        [pltpu.VMEM((ND * 64, others), BF16)],
    )(docs, docs_o, phase, amp, *all_dirs)

    state = [prox]
    scratch = [pltpu.VMEM((C, ND * ROWS), BF16), pltpu.VMEM((C, ND * ROWS), BF16)]
    for k in range(1, ITERS + 1):
        last = k == ITERS
        if last:
            outs = [shape(ROWS, C), shape(width, C)]
        else:
            outs = [
                shape(C, width),
                shape(C, width),
                shape(C, width),
                shape(7 * C + 8, ROWS),
                shape(2 * C + 8, ROWS),
            ]
        got = exchange(send)
        out = call(functools.partial(step_kernel, k, last), outs, scratch)(
            *got, high, low, far_high, far_low, inv, labels, weight, *state
        )
        if not last:
            *state, send = out
    return tuple(out)


def solution(mesh):
    in_specs = (P("doc", "feat"), P("doc", "feat"), P("feat"), P("feat"), P("doc"), P("doc"))
    out_specs = (P("doc", None), P("feat", None))
    return jax.shard_map(
        per_device, mesh=mesh, in_specs=in_specs, out_specs=out_specs, check_vma=False
    )
```

```python
import functools

import jax
import jax.numpy as jnp
from jax import lax
from jax.experimental import pallas as pl
from jax.experimental.pallas import tpu as pltpu
from jax.sharding import PartitionSpec as P

C = 128
ITERS = 3
NEWTON = 3
ND = 8
NF = 16
ROWS = 128
CHUNK = 256

shrink_level = 0.1
ratio_floor = 1e-06

AXES = ("doc", "feat")
F32 = jnp.float32
BF16 = jnp.bfloat16
SIN_TERMS = (
    -2.388494735328095e-08,
    2.752503405645257e-06,
    -0.00019840856839437038,
    0.008333330973982811,
    -0.1666666716337204,
    1.0,
)
INV_TWO_PI = 0.15915494309189535
PI_HIGH = 3.140625
PI_LOW = 0.0009676535897932


def nn(a, b):
    return lax.dot_general(a, b, (((1,), (0,)), ((), ())), preferred_element_type=F32)


def nt(a, b):
    return lax.dot_general(a, b, (((1,), (1,)), ((), ())), preferred_element_type=F32)


def tn(a, b):
    return lax.dot_general(a, b, (((0,), (0,)), ((), ())), preferred_element_type=F32)


def split(v):
    high = v.astype(BF16)
    return high, (v - high.astype(F32)).astype(BF16)


def product(a, b, dot=nn):
    ah, al = split(a)
    bh, bl = split(b)
    return dot(ah, bh) + (dot(ah, bl) + dot(al, bh))


def scaled_cos(angle, scale):
    turns = jnp.round(angle * INV_TWO_PI)
    half = (angle * 0.5 - turns * PI_HIGH) - turns * PI_LOW
    square = half * half
    series = SIN_TERMS[0]
    for term in SIN_TERMS[1:]:
        series = series * square + term
    sine = series * half
    return scale - (scale + scale) * (sine * sine)


def logistic_prox(target, signs, weight_ratio):
    current = target
    for _ in range(NEWTON):
        chance = 1.0 / (1.0 + jnp.exp(signs * current))
        gradient = current - target - weight_ratio * signs * chance
        current = current - gradient / (1.0 + weight_ratio * chance * (1.0 - chance))
    return current


def signs_of(labels_ref):
    labels = labels_ref[...]
    classes = lax.broadcasted_iota(jnp.int32, (C, ROWS), 0)
    return jnp.where(jnp.broadcast_to(labels, (C, ROWS)) == classes, 1.0, -1.0).astype(F32)


def total(v):
    return jnp.sum(jnp.sum(v, axis=0, keepdims=True), axis=1, keepdims=True)


def pack(values):
    lane = lax.broadcasted_iota(jnp.int32, (8, 128), 1)
    out = jnp.zeros((8, 128), F32)
    for k, v in enumerate(values):
        if v is not None:
            out = jnp.where(lane == k, jnp.broadcast_to(v, (8, 128)), out)
    return out


def inverse(matrix):
    n = matrix.shape[0]
    row_id = lax.broadcasted_iota(jnp.int32, (n, n), 0)
    col_id = lax.broadcasted_iota(jnp.int32, (n, n), 1)
    lane = lax.broadcasted_iota(jnp.int32, (1, n), 1)
    sub = lax.broadcasted_iota(jnp.int32, (n, 1), 0)
    m = matrix
    for k in range(n):
        recip = 1.0 / m[k : k + 1, k : k + 1]
        row = jnp.where(lane == k, recip, m[k : k + 1, :] * recip)
        col = jnp.where(sub == k, -1.0, m[:, k : k + 1])
        m = jnp.where((row_id == k) | (col_id == k), 0.0, m) - col * row
    return m


def doc_piece(docs_ref, slot):
    place = lax.axis_index("doc")
    block = ((place // 2 - slot // 2 + 4) % 4) * 2 + (place % 2 + slot % 2) % 2
    feat = lax.axis_index("feat")
    rows = docs_ref.shape[0] // NF
    pieces = []
    for half in range(2):
        source = 2 * block + half
        spot = ((feat // 4 - source // 4 + 4) % 4) * 4 + (feat % 4 - source % 4 + 4) % 4
        pieces.append(docs_ref[pl.ds(pl.multiple_of(rows * spot, rows), rows), :])
    return jnp.concatenate(pieces, axis=0)


def prepare_kernel(phase, amp, labels, weight, waves, facts, prox_ref):
    width = phase.shape[1]
    waves[0:1, :] = phase[...]
    waves[1:2, :] = amp[...] * (2.0 / width) ** 0.5
    signs = signs_of(labels)
    wide = jnp.broadcast_to(weight[...], (C, ROWS))
    facts[0:C, :] = signs
    facts[C : 2 * C, :] = wide
    prox_ref[...] = logistic_prox(jnp.zeros((C, ROWS), F32), signs, wide)


def own_kernel(docs, waves, prox, d0, d1, d2, d3, e0, e1, e2, e3, high, low, inv_h, inv_l, send):
    dirs = (d0, e0, d1, e1, d2, e2, d3, e3)
    left = jnp.concatenate([doc_piece(docs, s) for s in range(ND)], axis=0)
    width = waves.shape[1]
    gram = jnp.zeros((ROWS, 2 * ROWS), F32)
    for start in range(0, width, CHUNK):
        cols = pl.ds(start, CHUNK)
        right = jnp.concatenate([d[:, cols] for d in dirs], axis=0)
        angle = tn(left, right) + waves[0:1, cols]
        vh, vl = split(scaled_cos(angle, waves[1:2, cols]))
        high[:, cols] = vh
        low[:, cols] = vl
        gram = gram + nt(vh, jnp.concatenate([vh, vl], axis=0))
    cross = gram[:, ROWS:]
    row_id = lax.broadcasted_iota(jnp.int32, (ROWS, ROWS), 0)
    col_id = lax.broadcasted_iota(jnp.int32, (ROWS, ROWS), 1)
    whole = gram[:, :ROWS] + (cross + cross.T) + jnp.where(row_id == col_id, 1.0, 0.0)
    inv = inverse(whole)
    ih, il = split(inv)
    inv_h[...] = ih
    inv_l[...] = il
    right_side = prox[...] * (1.0 / NF)
    w = product(right_side, inv)
    send[0:C, :] = w
    send[C : C + 8, :] = pack([None, None, total(w * (right_side - w))])


def other_kernel(docs_z, docs_c, waves, d0, d1, d2, d3, e0, e1, e2, e3, high, low, left_ref):
    dirs = (d0, e0, d1, e1, d2, e2, d3, e3)
    width = waves.shape[1]
    blocks = [docs_c.at[b // 2] if b % 2 else docs_z.at[b // 2] for b in range(1, ND)]
    for s in range(ND):
        left_ref[s * 64 : s * 64 + 64, :] = jnp.concatenate(
            [doc_piece(block, s) for block in blocks], axis=1
        )

    def step(c, carry):
        cols = pl.ds(pl.multiple_of(c * CHUNK, CHUNK), CHUNK)
        right = jnp.concatenate([d[:, cols] for d in dirs], axis=0)
        scale = waves[1:2, cols]
        turn = waves[0:1, cols]
        for b in range(ND - 1):
            angle = tn(left_ref[:, b * ROWS : (b + 1) * ROWS], right) + turn
            vh, vl = split(scaled_cos(angle, scale))
            high[b * ROWS : (b + 1) * ROWS, cols] = vh
            low[b * ROWS : (b + 1) * ROWS, cols] = vl
        return carry

    lax.fori_loop(0, width // CHUNK, step, 0)


def spread_kernel(parts, near, cores, oh, ol, th, tl, *refs):
    outs, (tally, wide) = refs[:parts], refs[parts:]
    width = oh.shape[1]
    n_rows = near.shape[1]
    tail = jnp.zeros((8, ROWS), F32)
    for slot in range(ND):
        ref = (cores if slot % 2 else near).at[slot // 2]
        cols = pl.ds(slot * ROWS, ROWS)
        tail = tail + ref[n_rows - 8 : n_rows, :]
        for part in range(parts):
            qh, ql = split(ref[part * C : (part + 1) * C, :])
            wide[part * C : (part + 1) * C, cols] = qh
            wide[(parts + part) * C : (parts + part + 1) * C, cols] = ql
    tally[...] = tail
    count = parts * C

    def chunk(c, carry):
        cols = pl.ds(pl.multiple_of(c * CHUNK, CHUNK), CHUNK)
        both = nn(wide[:, ROWS:], th[:, cols]) + nn(wide[:, :ROWS], oh[:, cols])
        cross = nn(wide[:count, ROWS:], tl[:, cols]) + nn(wide[:count, :ROWS], ol[:, cols])
        result = both[:count] + (both[count:] + cross)
        for part in range(parts):
            outs[part][:, cols] = result[part * C : (part + 1) * C]
        return carry

    lax.fori_loop(0, width // CHUNK, chunk, 0)


def step_kernel(k, last, *refs):
    it = iter(refs)
    take = lambda n: [next(it) for _ in range(n)]
    feat_in = take(4)
    own, tally, facts = take(3)
    spread = take(1 if k == 1 else 2)
    if not last:
        oh, ol, inv_h, inv_l = take(4)
    if k == 1:
        prox_prev, = take(1)
    else:
        z_prev, v_prev, e_prev, small = take(4)
    if last:
        out_m, out_z = take(2)
    else:
        z_out, v_out, e_out, small_out, send = take(5)
    width = spread[0].shape[1]
    n_rows = own.shape[0]

    def feat_total(rows):
        return (feat_in[0][rows, :] + feat_in[1][rows, :]) + (feat_in[2][rows, :] + feat_in[3][rows, :])

    feat_scalars = feat_total(pl.ds(n_rows - 8, 8))[0:1, :]
    doc_scalars = tally[0:1, :]
    first = pl.ds(0, C)
    second = pl.ds(C, C)
    at = lambda row, n: row[:, n : n + 1]
    if k == 1:
        rho = jnp.ones((1, 1), F32)
        inv_g = None
        quad = at(doc_scalars, 2)
    else:
        rho_prev = small[7 * C : 7 * C + 1, 0:1]
        primal = at(feat_scalars, 0) + at(doc_scalars, 5)
        dual = rho_prev * rho_prev * (ND * at(feat_scalars, 1) + at(doc_scalars, 6))
        g = jnp.sqrt(jnp.sqrt((primal + ratio_floor) / (dual + ratio_floor)))
        rho = rho_prev * g
        inv_g = 1.0 / g
        quad = at(doc_scalars, 2) + inv_g * (at(doc_scalars, 3) + inv_g * at(doc_scalars, 4))

    limit = shrink_level / (rho * ND)

    def chunk(c, carry):
        az, norm_p, norm_d = carry
        cols = pl.ds(pl.multiple_of(c * CHUNK, CHUNK), CHUNK)
        if k == 1:
            v = qsum = spread[0][:, cols]
            target = v * (1.0 / ND)
            z = target - jnp.clip(target, -limit, limit)
            e = -z
            p = e
        else:
            qsum = spread[0][:, cols] + spread[1][:, cols] * inv_g
            v = qsum + v_prev[:, cols] * inv_g
            z_old = z_prev[:, cols]
            target = z_old + v * (1.0 / ND)
            z = target - jnp.clip(target, -limit, limit)
            e = z_old - z
            p = e - e_prev[:, cols] * inv_g
        if last:
            out_z[cols, :] = (z * float(NF)).T
            return carry
        v_out[:, cols] = v
        z_out[:, cols] = z
        e_out[:, cols] = e
        norm_p = norm_p + jnp.sum(p * (ND * p + 2.0 * qsum), axis=0, keepdims=True)
        norm_d = norm_d + jnp.sum(e * e, axis=0, keepdims=True)
        zh, zl = split(z)
        az2 = nt(jnp.concatenate([zh, zl], axis=0), oh[:, cols])
        az = az + ((az2[:C] + az2[C:]) + nt(zh, ol[:, cols]))
        return az, norm_p, norm_d

    init = (jnp.zeros((C, ROWS), F32), jnp.zeros((1, CHUNK), F32), jnp.zeros((1, CHUNK), F32))
    az, norm_p, norm_d = lax.fori_loop(0, width // CHUNK, chunk, init)

    signs = facts[0:C, :]
    ratio = facts[C : 2 * C, :] / rho
    w_sum = feat_total(first)
    if k == 1:
        m_prev = prox_prev[...]
    else:
        m_prev = small[0:C, :]
        w_sum = w_sum + (feat_total(second) + small[C : 2 * C, :]) * inv_g
    target = m_prev - w_sum
    margins = logistic_prox(target, signs, ratio)
    if last:
        out_m[...] = margins.T
        return
    if k == 1:
        b_prev = jnp.zeros((C, ROWS), F32)
        w = own[first, :]
        y = m_prev * (1.0 / NF) - w
        az_prev = jnp.zeros((C, ROWS), F32)
    else:
        b_prev = small[2 * C : 3 * C, :] * inv_g
        w = own[first, :] + (own[second, :] + small[3 * C : 4 * C, :]) * inv_g
        y = small[4 * C : 5 * C, :] + (m_prev - b_prev - small[5 * C : 6 * C, :]) * (1.0 / NF) - w
        az_prev = small[6 * C : 7 * C, :]
    b_new = target - margins
    sums = target - b_prev
    small_out[0:C, :] = margins
    small_out[C : 2 * C, :] = w_sum
    small_out[2 * C : 3 * C, :] = b_new
    small_out[3 * C : 4 * C, :] = w
    small_out[4 * C : 5 * C, :] = y
    small_out[5 * C : 6 * C, :] = sums
    small_out[6 * C : 7 * C, :] = az
    small_out[7 * C : 7 * C + 8, :] = jnp.broadcast_to(rho, (8, 128))
    ru = y + (margins - sums) * (1.0 / NF) - az
    rv = az_prev - az - w - b_new * (1.0 / NF)
    rh, rl = split(jnp.concatenate([ru, rv], axis=0))
    ih = inv_h[...]
    solved = nn(rh, ih) + (nn(rl, ih) + nn(rh, inv_l[...]))
    u = solved[:C]
    v2 = solved[C:]
    send[0:C, :] = u
    send[C : 2 * C, :] = v2
    part = rv - v2
    gap = sums - margins
    move = margins - m_prev
    send[2 * C : 2 * C + 8, :] = pack(
        [
            jnp.sum(norm_p, axis=1, keepdims=True) + quad,
            jnp.sum(norm_d, axis=1, keepdims=True),
            total(u * (ru - u)),
            2.0 * total(u * part),
            total(v2 * part),
            total(gap * gap),
            total(move * move),
        ]
    )


def table(move):
    pairs = []
    for d in range(ND):
        for f in range(NF):
            z, core, x, y = d // 2, d % 2, f // 4, f % 4
            z2, core2, x2, y2 = move(z, core, x, y)
            pairs.append((d * NF + f, ((z2 % 4) * 2 + core2) * NF + (x2 % 4) * 4 + y2 % 4))
    return pairs


def along_y(v, k):
    return lax.ppermute(v, AXES, table(lambda z, c, x, y: (z, c, x, y + k)))


def along_x(v, k):
    return lax.ppermute(v, AXES, table(lambda z, c, x, y: (z, c, x + k, y)))


def along_z(v, k):
    return lax.ppermute(v, AXES, table(lambda z, c, x, y: (z + k, c, x, y)))


def across(v):
    return lax.ppermute(v, AXES, table(lambda z, c, x, y: (z, 1 - c, x, y)))


def call(body, outs, scratch=(), flops=0, limit=24):
    return pl.pallas_call(
        body,
        out_shape=outs,
        scratch_shapes=list(scratch),
        cost_estimate=pl.CostEstimate(flops=flops, bytes_accessed=0, transcendentals=0),
        compiler_params=pltpu.CompilerParams(vmem_limit_bytes=limit * 1024 * 1024),
    )


def shape(*dims, dtype=F32):
    return jax.ShapeDtypeStruct(dims, dtype)


def gather_line(v, move):
    return [v] + [move(v, k) for k in (1, 2, 3)]


def per_device(documents, directions, phase, amplitude, doc_weight, labels):
    width = directions.shape[1]
    docs_y = jnp.concatenate(gather_line(documents.T, along_y), axis=0)
    docs = jnp.concatenate(gather_line(docs_y, along_x), axis=0)
    dirs = gather_line(directions, along_z)
    dirs_other = [across(d) for d in dirs]
    waves, facts, prox = call(
        prepare_kernel, [shape(8, width), shape(2 * C, ROWS), shape(C, ROWS)]
    )(
        phase.reshape(1, width),
        amplitude.reshape(1, width),
        labels.reshape(1, ROWS),
        doc_weight.reshape(1, ROWS),
    )
    all_dirs = dirs + dirs_other
    high, low, inv_h, inv_l, send = call(
        own_kernel,
        [
            shape(ROWS, width, dtype=BF16),
            shape(ROWS, width, dtype=BF16),
            shape(ROWS, ROWS, dtype=BF16),
            shape(ROWS, ROWS, dtype=BF16),
            shape(C + 8, ROWS),
        ],
    )(docs, waves, prox, *all_dirs)

    docs_z = jnp.stack(gather_line(docs, along_z))
    docs_c = across(docs_z)
    others = (ND - 1) * ROWS
    far_high, far_low = call(
        other_kernel,
        [shape(others, width, dtype=BF16), shape(others, width, dtype=BF16)],
        [pltpu.VMEM((ND * 64, others), BF16)],
        flops=10**10,
    )(docs_z, docs_c, waves, *all_dirs)

    state = [prox]
    for k in range(1, ITERS + 1):
        last = k == ITERS
        parts = 1 if k == 1 else 2
        if last:
            outs = [shape(ROWS, C), shape(width, C)]
            mats = []
        else:
            outs = [
                shape(C, width),
                shape(C, width),
                shape(C, width),
                shape(7 * C + 8, ROWS),
                shape(2 * C + 8, ROWS),
            ]
            mats = [high, low, inv_h, inv_l]
        zs = gather_line(send, along_z)
        ys = gather_line(send, along_y)
        zs, ys = lax.optimization_barrier((zs, ys))
        near = jnp.stack(zs)
        cores = across(near)
        line = (ys[0] + ys[1]) + (ys[2] + ys[3])
        xs = gather_line(line, along_x)
        *spread, tally = call(
            functools.partial(spread_kernel, parts),
            [shape(C, width)] * parts + [shape(8, ROWS)],
            [pltpu.VMEM((2 * parts * C, ND * ROWS), BF16)],
            flops=4 * 10**9,
        )(near, cores, high, low, far_high, far_low)
        out = call(functools.partial(step_kernel, k, last), outs)(
            *xs, send, tally, facts, *spread, *mats, *state
        )
        if not last:
            *state, send = out
    return tuple(out)


def solution(mesh):
    in_specs = (P("doc", "feat"), P("doc", "feat"), P("feat"), P("feat"), P("doc"), P("doc"))
    out_specs = (P("doc", None), P("feat", None))
    return jax.shard_map(
        per_device, mesh=mesh, in_specs=in_specs, out_specs=out_specs, check_vma=False
    )
```

```python
import functools

import jax
import jax.numpy as jnp
from jax import lax
from jax.experimental import pallas as pl
from jax.experimental.pallas import tpu as pltpu
from jax.sharding import PartitionSpec as P

C = 128
ITERS = 3
NEWTON = 3
ND = 8
NF = 16
ROWS = 128
CHUNK = 256

shrink_level = 0.1
ratio_floor = 1e-06

AXES = ("doc", "feat")
F32 = jnp.float32
BF16 = jnp.bfloat16
SIN_TERMS = (
    0.07765547442052619,
    -0.5982903290573769,
    2.5500773950715985,
    -5.1677100781672785,
    3.1415926400973193,
)
INV_TWO_PI = 0.15915494309189535


def nn(a, b):
    return lax.dot_general(a, b, (((1,), (0,)), ((), ())), preferred_element_type=F32)


def nt(a, b):
    return lax.dot_general(a, b, (((1,), (1,)), ((), ())), preferred_element_type=F32)


def split(v):
    high = v.astype(BF16)
    return high, (v - high.astype(F32)).astype(BF16)


def product(a, b, dot=nn):
    ah, al = split(a)
    bh, bl = split(b)
    return dot(ah, bh) + (dot(ah, bl) + dot(al, bh))


def split3(v):
    high = v.astype(BF16)
    rest = v - high.astype(F32)
    mid = rest.astype(BF16)
    return high, mid, (rest - mid.astype(F32)).astype(BF16)


def full_product(a, b):
    ah, am, al = split3(a)
    bh, bm, bl = split3(b)
    small = nn(am, bm) + (nn(ah, bl) + nn(al, bh))
    return nn(ah, bh) + ((nn(ah, bm) + nn(am, bh)) + small)


def feature_values(dots, waves, cols):
    turns = dots * INV_TWO_PI + waves[0:1, cols]
    part = turns - jnp.round(turns)
    square = part * part
    series = SIN_TERMS[0]
    for term in SIN_TERMS[1:]:
        series = series * square + term
    sine = series * part
    return split(waves[1:2, cols] - waves[2:3, cols] * (sine * sine))


def logistic_prox(target, signs, weight_ratio):
    current = target
    for _ in range(NEWTON):
        chance = 1.0 / (1.0 + jnp.exp(signs * current))
        gradient = current - target - weight_ratio * signs * chance
        current = current - gradient / (1.0 + weight_ratio * chance * (1.0 - chance))
    return current


def signs_of(labels_ref):
    labels = labels_ref[...]
    classes = lax.broadcasted_iota(jnp.int32, (C, ROWS), 0)
    return jnp.where(jnp.broadcast_to(labels, (C, ROWS)) == classes, 1.0, -1.0).astype(F32)


def total(v):
    return jnp.sum(jnp.sum(v, axis=0, keepdims=True), axis=1, keepdims=True)


def pack(values):
    lane = lax.broadcasted_iota(jnp.int32, (8, 128), 1)
    out = jnp.zeros((8, 128), F32)
    for k, v in enumerate(values):
        if v is not None:
            out = jnp.where(lane == k, jnp.broadcast_to(v, (8, 128)), out)
    return out


def inverse(matrix):
    n = matrix.shape[0]
    row_id = lax.broadcasted_iota(jnp.int32, (n, n), 0)
    col_id = lax.broadcasted_iota(jnp.int32, (n, n), 1)
    unit = jnp.where(row_id == col_id, 1.0, 0.0)
    top = jnp.max(jnp.sum(jnp.abs(matrix), axis=0))
    alpha = 2.0 / (top + 1.0)
    residual = unit - matrix * alpha
    guess = unit * alpha
    shrink = (top - 1.0) * (0.5 * alpha)

    def wide(carry):
        return carry[2] > 1e-4

    def double(carry):
        x, r, rate = carry
        rh, rl = split(r)
        xh, xl = split(x)
        both = nn(jnp.concatenate([xh, rh, xl, rl], axis=0), rh)
        cross = nn(jnp.concatenate([xh, rh], axis=0), rl)
        both = both[: 2 * n] + (both[2 * n :] + cross)
        return x + both[:n], both[n:], rate * rate

    guess, _, _ = lax.while_loop(wide, double, (guess, residual, shrink))

    def inexact(carry):
        return carry[1] > 1e-3

    def correct(carry):
        x, _ = carry
        r = unit - full_product(matrix, x)
        size = jnp.max(jnp.sum(jnp.abs(r), axis=0))
        return x + product(x, r), size

    guess, _ = lax.while_loop(inexact, correct, (guess, jnp.float32(1.0)))
    return guess


def doc_piece(docs_ref, slot):
    place = lax.axis_index("doc")
    block = ((place // 2 - slot // 2 + 4) % 4) * 2 + (place % 2 + slot % 2) % 2
    feat = lax.axis_index("feat")
    rows = docs_ref.shape[0] // NF
    pieces = []
    for half in range(2):
        source = 2 * block + half
        spot = source
        pieces.append(docs_ref[pl.ds(pl.multiple_of(rows * spot, rows), rows), :])
    return jnp.concatenate(pieces, axis=0)


def prepare_kernel(phase, amp, labels, weight, dirs, waves, facts, prox_ref, copied):
    copied[...] = dirs[...]
    width = phase.shape[1]
    scale = amp[...] * (2.0 / width) ** 0.5
    waves[0:1, :] = phase[...] * INV_TWO_PI
    waves[1:2, :] = scale
    waves[2:3, :] = scale + scale
    signs = signs_of(labels)
    wide = jnp.broadcast_to(weight[...], (C, ROWS))
    facts[0:C, :] = signs
    facts[C : 2 * C, :] = wide
    prox_ref[...] = logistic_prox(jnp.zeros((C, ROWS), F32), signs, wide)


def own_kernel(docs, waves, prox, d0, d1, d2, d3, e0, e1, e2, e3, high, low, inv_h, inv_l, send):
    dirs = (d0, e0, d1, e1, d2, e2, d3, e3)
    left = jnp.concatenate([doc_piece(docs, s) for s in range(ND)], axis=0)
    left = left.astype(F32).T.astype(BF16)
    width = waves.shape[1]
    gram = jnp.zeros((ROWS, 2 * ROWS), F32)
    for start in range(0, width, CHUNK):
        cols = pl.ds(start, CHUNK)
        right = jnp.concatenate([d[:, cols] for d in dirs], axis=0)
        vh, vl = feature_values(nn(left, right), waves, cols)
        high[:, cols] = vh
        low[:, cols] = vl
        gram = gram + nt(vh, jnp.concatenate([vh, vl], axis=0))
    cross = gram[:, ROWS:]
    row_id = lax.broadcasted_iota(jnp.int32, (ROWS, ROWS), 0)
    col_id = lax.broadcasted_iota(jnp.int32, (ROWS, ROWS), 1)
    whole = gram[:, :ROWS] + (cross + cross.T) + jnp.where(row_id == col_id, 1.0, 0.0)
    inv = inverse(whole)
    ih, il = split(inv)
    inv_h[...] = ih
    inv_l[...] = il
    right_side = prox[...] * (1.0 / NF)
    w = product(right_side, inv)
    send[0:C, :] = w
    send[C : C + 8, :] = pack([None, None, total(w * (right_side - w))])


def other_kernel(docs_z, docs_c, own_h, own_l, waves, d0, d1, d2, d3, e0, e1, e2, e3, high, low, left_ref):
    high[0:ROWS, :] = own_h[...]
    low[0:ROWS, :] = own_l[...]
    dirs = (d0, e0, d1, e1, d2, e2, d3, e3)
    width = waves.shape[1]
    blocks = [docs_c.at[b // 2] if b % 2 else docs_z.at[b // 2] for b in range(1, ND)]
    for b, block in enumerate(blocks):
        left = jnp.concatenate([doc_piece(block, s) for s in range(ND)], axis=0)
        left_ref[b * ROWS : (b + 1) * ROWS, :] = left.astype(F32).T.astype(BF16)

    def step(c, carry):
        cols = pl.ds(pl.multiple_of(c * CHUNK, CHUNK), CHUNK)
        right = jnp.concatenate([d[:, cols] for d in dirs], axis=0)
        for b in range(ND - 1):
            dots = nn(left_ref[b * ROWS : (b + 1) * ROWS, :], right)
            vh, vl = feature_values(dots, waves, cols)
            high[(b + 1) * ROWS : (b + 2) * ROWS, cols] = vh
            low[(b + 1) * ROWS : (b + 2) * ROWS, cols] = vl
        return carry

    lax.fori_loop(0, width // CHUNK, step, 0)


def spread_kernel(parts, near, cores, high, low, *refs):
    outs, (tally, wide) = refs[:parts], refs[parts:]
    width = high.shape[1]
    n_rows = near.shape[1]
    tail = jnp.zeros((8, ROWS), F32)
    for slot in range(ND):
        ref = (cores if slot % 2 else near).at[slot // 2]
        cols = pl.ds(slot * ROWS, ROWS)
        tail = tail + ref[n_rows - 8 : n_rows, :]
        for part in range(parts):
            qh, ql = split(ref[part * C : (part + 1) * C, :])
            wide[part * C : (part + 1) * C, cols] = qh
            wide[(parts + part) * C : (parts + part + 1) * C, cols] = ql
    tally[...] = tail
    count = parts * C

    def chunk(c, carry):
        cols = pl.ds(pl.multiple_of(c * CHUNK, CHUNK), CHUNK)
        both = nn(wide[...], high[:, cols])
        cross = nn(wide[:count, :], low[:, cols])
        result = both[:count] + (both[count:] + cross)
        for part in range(parts):
            outs[part][:, cols] = result[part * C : (part + 1) * C]
        return carry

    lax.fori_loop(0, width // CHUNK, chunk, 0)


def step_kernel(k, last, *refs):
    it = iter(refs)
    take = lambda n: [next(it) for _ in range(n)]
    feat_in = take(4)
    own, tally, facts = take(3)
    spread = take(1 if k == 1 else 2)
    if not last:
        oh, ol, inv_h, inv_l = take(4)
    if k == 1:
        prox_prev, = take(1)
    else:
        z_prev, v_prev, e_prev, small = take(4)
    if last:
        out_m, out_z = take(2)
    else:
        z_out, v_out, e_out, small_out, send = take(5)
    width = spread[0].shape[1]
    n_rows = own.shape[0]

    def feat_total(rows):
        return (feat_in[0][rows, :] + feat_in[1][rows, :]) + (feat_in[2][rows, :] + feat_in[3][rows, :])

    feat_scalars = feat_total(pl.ds(n_rows - 8, 8))[0:1, :]
    doc_scalars = tally[0:1, :]
    first = pl.ds(0, C)
    second = pl.ds(C, C)
    at = lambda row, n: row[:, n : n + 1]
    if k == 1:
        rho = jnp.ones((1, 1), F32)
        inv_g = None
        quad = at(doc_scalars, 2)
    else:
        rho_prev = small[7 * C : 7 * C + 1, 0:1]
        primal = at(feat_scalars, 0) + at(doc_scalars, 5)
        dual = rho_prev * rho_prev * (ND * at(feat_scalars, 1) + at(doc_scalars, 6))
        g = jnp.sqrt(jnp.sqrt((primal + ratio_floor) / (dual + ratio_floor)))
        rho = rho_prev * g
        inv_g = 1.0 / g
        quad = at(doc_scalars, 2) + inv_g * (at(doc_scalars, 3) + inv_g * at(doc_scalars, 4))

    limit = shrink_level / (rho * ND)

    def chunk(c, carry):
        az, norm_p, norm_d = carry
        cols = pl.ds(pl.multiple_of(c * CHUNK, CHUNK), CHUNK)
        if k == 1:
            v = qsum = spread[0][:, cols]
            target = v * (1.0 / ND)
            z = target - jnp.clip(target, -limit, limit)
            e = -z
            p = e
        else:
            qsum = spread[0][:, cols] + spread[1][:, cols] * inv_g
            v = qsum + v_prev[:, cols] * inv_g
            z_old = z_prev[:, cols]
            target = z_old + v * (1.0 / ND)
            z = target - jnp.clip(target, -limit, limit)
            e = z_old - z
            p = e - e_prev[:, cols] * inv_g
        if last:
            out_z[cols, :] = (z * float(NF)).T
            return carry
        v_out[:, cols] = v
        z_out[:, cols] = z
        e_out[:, cols] = e
        norm_p = norm_p + jnp.sum(p * (ND * p + 2.0 * qsum), axis=0, keepdims=True)
        norm_d = norm_d + jnp.sum(e * e, axis=0, keepdims=True)
        zh, zl = split(z)
        az2 = nt(jnp.concatenate([zh, zl], axis=0), oh[0:ROWS, cols])
        az = az + ((az2[:C] + az2[C:]) + nt(zh, ol[0:ROWS, cols]))
        return az, norm_p, norm_d

    init = (jnp.zeros((C, ROWS), F32), jnp.zeros((1, CHUNK), F32), jnp.zeros((1, CHUNK), F32))
    az, norm_p, norm_d = lax.fori_loop(0, width // CHUNK, chunk, init)

    signs = facts[0:C, :]
    ratio = facts[C : 2 * C, :] / rho
    w_sum = feat_total(first)
    if k == 1:
        m_prev = prox_prev[...]
    else:
        m_prev = small[0:C, :]
        w_sum = w_sum + (feat_total(second) + small[C : 2 * C, :]) * inv_g
    target = m_prev - w_sum
    margins = logistic_prox(target, signs, ratio)
    if last:
        out_m[...] = margins.T
        return
    if k == 1:
        b_prev = jnp.zeros((C, ROWS), F32)
        w = own[first, :]
        y = m_prev * (1.0 / NF) - w
        az_prev = jnp.zeros((C, ROWS), F32)
    else:
        b_prev = small[2 * C : 3 * C, :] * inv_g
        w = own[first, :] + (own[second, :] + small[3 * C : 4 * C, :]) * inv_g
        y = small[4 * C : 5 * C, :] + (m_prev - b_prev - small[5 * C : 6 * C, :]) * (1.0 / NF) - w
        az_prev = small[6 * C : 7 * C, :]
    b_new = target - margins
    sums = target - b_prev
    small_out[0:C, :] = margins
    small_out[C : 2 * C, :] = w_sum
    small_out[2 * C : 3 * C, :] = b_new
    small_out[3 * C : 4 * C, :] = w
    small_out[4 * C : 5 * C, :] = y
    small_out[5 * C : 6 * C, :] = sums
    small_out[6 * C : 7 * C, :] = az
    small_out[7 * C : 7 * C + 8, :] = jnp.broadcast_to(rho, (8, 128))
    ru = y + (margins - sums) * (1.0 / NF) - az
    rv = az_prev - az - w - b_new * (1.0 / NF)
    rh, rl = split(jnp.concatenate([ru, rv], axis=0))
    ih = inv_h[...]
    solved = nn(rh, ih) + (nn(rl, ih) + nn(rh, inv_l[...]))
    u = solved[:C]
    v2 = solved[C:]
    send[0:C, :] = u
    send[C : 2 * C, :] = v2
    part = rv - v2
    gap = sums - margins
    move = margins - m_prev
    send[2 * C : 2 * C + 8, :] = pack(
        [
            jnp.sum(norm_p, axis=1, keepdims=True) + quad,
            jnp.sum(norm_d, axis=1, keepdims=True),
            total(u * (ru - u)),
            2.0 * total(u * part),
            total(v2 * part),
            total(gap * gap),
            total(move * move),
        ]
    )


def table(move):
    pairs = []
    for d in range(ND):
        for f in range(NF):
            z, core, x, y = d // 2, d % 2, f // 4, f % 4
            z2, core2, x2, y2 = move(z, core, x, y)
            pairs.append((d * NF + f, ((z2 % 4) * 2 + core2) * NF + (x2 % 4) * 4 + y2 % 4))
    return pairs


def along_y(v, k):
    return lax.ppermute(v, AXES, table(lambda z, c, x, y: (z, c, x, y + k)))


def along_x(v, k):
    return lax.ppermute(v, AXES, table(lambda z, c, x, y: (z, c, x + k, y)))


def along_z(v, k):
    return lax.ppermute(v, AXES, table(lambda z, c, x, y: (z + k, c, x, y)))


def across(v):
    return lax.ppermute(v, AXES, table(lambda z, c, x, y: (z, 1 - c, x, y)))


def call(body, outs, scratch=(), flops=0, limit=24):
    return pl.pallas_call(
        body,
        out_shape=outs,
        scratch_shapes=list(scratch),
        cost_estimate=pl.CostEstimate(flops=flops, bytes_accessed=0, transcendentals=0),
        compiler_params=pltpu.CompilerParams(vmem_limit_bytes=limit * 1024 * 1024),
    )


def shape(*dims, dtype=F32):
    return jax.ShapeDtypeStruct(dims, dtype)


def gather_line(v, move):
    return [v] + [move(v, k) for k in (1, 2, 3)]


def per_device(documents, directions, phase, amplitude, doc_weight, labels):
    width = directions.shape[1]
    dirs = gather_line(directions, along_z)
    docs = lax.all_to_all(
        jnp.broadcast_to(documents.T[None], (NF,) + documents.T.shape), "feat", 0, 0
    )
    waves, facts, prox, copied = call(
        prepare_kernel,
        [
            shape(8, width),
            shape(2 * C, ROWS),
            shape(C, ROWS),
            shape(*directions.shape, dtype=BF16),
        ],
    )(
        phase.reshape(1, width),
        amplitude.reshape(1, width),
        labels.reshape(1, ROWS),
        doc_weight.reshape(1, ROWS),
        directions,
    )
    dirs[0] = copied
    dirs, docs, waves, facts, prox = lax.optimization_barrier((dirs, docs, waves, facts, prox))
    dirs_other = [across(d) for d in dirs]
    docs = docs.reshape(-1, ROWS)
    all_dirs = dirs + dirs_other
    high, low, inv_h, inv_l, send = call(
        own_kernel,
        [
            shape(ROWS, width, dtype=BF16),
            shape(ROWS, width, dtype=BF16),
            shape(ROWS, ROWS, dtype=BF16),
            shape(ROWS, ROWS, dtype=BF16),
            shape(C + 8, ROWS),
        ],
    )(docs, waves, prox, *all_dirs)

    docs_z, send = lax.optimization_barrier((gather_line(docs, along_z), send))
    docs_z = jnp.stack(docs_z)
    docs_c = across(docs_z)
    every = ND * ROWS
    high, low = call(
        other_kernel,
        [shape(every, width, dtype=BF16), shape(every, width, dtype=BF16)],
        [pltpu.VMEM((every - ROWS, docs.shape[0]), BF16)],
        flops=10**10,
    )(docs_z, docs_c, high, low, waves, *all_dirs)

    state = [prox]
    for k in range(1, ITERS + 1):
        last = k == ITERS
        parts = 1 if k == 1 else 2
        if last:
            outs = [shape(ROWS, C), shape(width, C)]
            mats = []
        else:
            outs = [
                shape(C, width),
                shape(C, width),
                shape(C, width),
                shape(7 * C + 8, ROWS),
                shape(2 * C + 8, ROWS),
            ]
            mats = [high, low, inv_h, inv_l]
        zs = gather_line(send, along_z)
        ys = gather_line(send, along_y)
        if k == 1:
            zs, ys, high, low = lax.optimization_barrier((zs, ys, high, low))
        else:
            zs, ys = lax.optimization_barrier((zs, ys))
        near = jnp.stack(zs)
        cores = across(near)
        line = (ys[0] + ys[1]) + (ys[2] + ys[3])
        xs = gather_line(line, along_x)
        *spread, tally = call(
            functools.partial(spread_kernel, parts),
            [shape(C, width)] * parts + [shape(8, ROWS)],
            [pltpu.VMEM((2 * parts * C, ND * ROWS), BF16)],
            flops=4 * 10**9,
        )(near, cores, high, low)
        out = call(functools.partial(step_kernel, k, last), outs)(
            *xs, send, tally, facts, *spread, *mats, *state
        )
        if not last:
            *state, send = out
    return tuple(out)


def solution(mesh):
    in_specs = (P("doc", "feat"), P("doc", "feat"), P("feat"), P("feat"), P("doc"), P("doc"))
    out_specs = (P("doc", None), P("feat", None))
    return jax.shard_map(
        per_device, mesh=mesh, in_specs=in_specs, out_specs=out_specs, check_vma=False
    )
```

```python
import functools

import jax
import jax.numpy as jnp
from jax import lax
from jax.experimental import pallas as pl
from jax.experimental.pallas import tpu as pltpu
from jax.sharding import PartitionSpec as P

C = 128
ITERS = 3
NEWTON = 3
ND = 8
NF = 16
ROWS = 128
CHUNK = 256

shrink_level = 0.1
ratio_floor = 1e-06

AXES = ("doc", "feat")
F32 = jnp.float32
BF16 = jnp.bfloat16
SIN_TERMS = (
    0.07765547442052619,
    -0.5982903290573769,
    2.5500773950715985,
    -5.1677100781672785,
    3.1415926400973193,
)
INV_TWO_PI = 0.15915494309189535


def nn(a, b):
    return lax.dot_general(a, b, (((1,), (0,)), ((), ())), preferred_element_type=F32)


def nt(a, b):
    return lax.dot_general(a, b, (((1,), (1,)), ((), ())), preferred_element_type=F32)


def split(v):
    high = v.astype(BF16)
    return high, (v - high.astype(F32)).astype(BF16)


def product(a, b, dot=nn):
    ah, al = split(a)
    bh, bl = split(b)
    return dot(ah, bh) + (dot(ah, bl) + dot(al, bh))


def split3(v):
    high = v.astype(BF16)
    rest = v - high.astype(F32)
    mid = rest.astype(BF16)
    return high, mid, (rest - mid.astype(F32)).astype(BF16)


def full_product(a, b):
    ah, am, al = split3(a)
    bh, bm, bl = split3(b)
    small = nn(am, bm) + (nn(ah, bl) + nn(al, bh))
    return nn(ah, bh) + ((nn(ah, bm) + nn(am, bh)) + small)


def feature_values(dots, waves, cols):
    turns = dots * INV_TWO_PI + waves[0:1, cols]
    part = turns - jnp.round(turns)
    square = part * part
    series = SIN_TERMS[0]
    for term in SIN_TERMS[1:]:
        series = series * square + term
    sine = series * part
    return split(waves[1:2, cols] - waves[2:3, cols] * (sine * sine))


def logistic_prox(target, signs, weight_ratio):
    current = target
    for _ in range(NEWTON):
        chance = 1.0 / (1.0 + jnp.exp(signs * current))
        gradient = current - target - weight_ratio * signs * chance
        current = current - gradient / (1.0 + weight_ratio * chance * (1.0 - chance))
    return current


def signs_of(labels_ref):
    labels = labels_ref[...]
    classes = lax.broadcasted_iota(jnp.int32, (C, ROWS), 0)
    return jnp.where(jnp.broadcast_to(labels, (C, ROWS)) == classes, 1.0, -1.0).astype(F32)


def total(v):
    return jnp.sum(jnp.sum(v, axis=0, keepdims=True), axis=1, keepdims=True)


def pack(values):
    lane = lax.broadcasted_iota(jnp.int32, (8, 128), 1)
    out = jnp.zeros((8, 128), F32)
    for k, v in enumerate(values):
        if v is not None:
            out = jnp.where(lane == k, jnp.broadcast_to(v, (8, 128)), out)
    return out


def inverse(matrix):
    n = matrix.shape[0]
    row_id = lax.broadcasted_iota(jnp.int32, (n, n), 0)
    col_id = lax.broadcasted_iota(jnp.int32, (n, n), 1)
    unit = jnp.where(row_id == col_id, 1.0, 0.0)
    top = jnp.max(jnp.sum(jnp.abs(matrix), axis=0))
    alpha = 2.0 / (top + 1.0)
    residual = unit - matrix * alpha
    guess = unit * alpha
    shrink = (top - 1.0) * (0.5 * alpha)

    def wide(carry):
        return carry[2] > 1e-4

    def double(carry):
        x, r, rate = carry
        rh, rl = split(r)
        xh, xl = split(x)
        both = nn(jnp.concatenate([xh, rh, xl, rl], axis=0), rh)
        cross = nn(jnp.concatenate([xh, rh], axis=0), rl)
        both = both[: 2 * n] + (both[2 * n :] + cross)
        return x + both[:n], both[n:], rate * rate

    guess, _, _ = lax.while_loop(wide, double, (guess, residual, shrink))

    def inexact(carry):
        return carry[1] > 1e-3

    def correct(carry):
        x, _ = carry
        r = unit - full_product(matrix, x)
        size = jnp.max(jnp.sum(jnp.abs(r), axis=0))
        return x + product(x, r), size

    guess, _ = lax.while_loop(inexact, correct, (guess, jnp.float32(1.0)))
    return guess


def doc_piece(docs_ref, slot):
    place = lax.axis_index("doc")
    block = ((place // 2 - slot // 2 + 4) % 4) * 2 + (place % 2 + slot % 2) % 2
    feat = lax.axis_index("feat")
    rows = docs_ref.shape[0] // NF
    pieces = []
    for half in range(2):
        source = 2 * block + half
        spot = source
        pieces.append(docs_ref[pl.ds(pl.multiple_of(rows * spot, rows), rows), :])
    return jnp.concatenate(pieces, axis=0)


def prepare_kernel(phase, amp, labels, weight, dirs, waves, facts, prox_ref, copied):
    copied[...] = dirs[...]
    width = phase.shape[1]
    scale = amp[...] * (2.0 / width) ** 0.5
    waves[0:1, :] = phase[...] * INV_TWO_PI
    waves[1:2, :] = scale
    waves[2:3, :] = scale + scale
    signs = signs_of(labels)
    wide = jnp.broadcast_to(weight[...], (C, ROWS))
    facts[0:C, :] = signs
    facts[C : 2 * C, :] = wide
    prox_ref[...] = logistic_prox(jnp.zeros((C, ROWS), F32), signs, wide)


def own_kernel(docs, waves, prox, d0, d1, d2, d3, e0, e1, e2, e3, high, low, inv_h, inv_l, send):
    dirs = (d0, e0, d1, e1, d2, e2, d3, e3)
    left = jnp.concatenate([doc_piece(docs, s) for s in range(ND)], axis=0)
    left = left.astype(F32).T.astype(BF16)
    width = waves.shape[1]
    gram = jnp.zeros((ROWS, 2 * ROWS), F32)
    for start in range(0, width, CHUNK):
        cols = pl.ds(start, CHUNK)
        right = jnp.concatenate([d[:, cols] for d in dirs], axis=0)
        vh, vl = feature_values(nn(left, right), waves, cols)
        high[:, cols] = vh
        low[:, cols] = vl
        gram = gram + nt(vh, jnp.concatenate([vh, vl], axis=0))
    cross = gram[:, ROWS:]
    row_id = lax.broadcasted_iota(jnp.int32, (ROWS, ROWS), 0)
    col_id = lax.broadcasted_iota(jnp.int32, (ROWS, ROWS), 1)
    whole = gram[:, :ROWS] + (cross + cross.T) + jnp.where(row_id == col_id, 1.0, 0.0)
    inv = inverse(whole)
    ih, il = split(inv)
    inv_h[...] = ih
    inv_l[...] = il
    right_side = prox[...] * (1.0 / NF)
    w = product(right_side, inv)
    send[0:C, :] = w
    send[C : C + 8, :] = pack([None, None, total(w * (right_side - w))])


def other_kernel(docs_z, docs_c, own_h, own_l, waves, d0, d1, d2, d3, e0, e1, e2, e3, high, low, left_ref):
    high[0:ROWS, :] = own_h[...]
    low[0:ROWS, :] = own_l[...]
    dirs = (d0, e0, d1, e1, d2, e2, d3, e3)
    width = waves.shape[1]
    blocks = [docs_c.at[b // 2] if b % 2 else docs_z.at[b // 2] for b in range(1, ND)]
    for b, block in enumerate(blocks):
        left = jnp.concatenate([doc_piece(block, s) for s in range(ND)], axis=0)
        left_ref[b * ROWS : (b + 1) * ROWS, :] = left.astype(F32).T.astype(BF16)

    def step(c, carry):
        cols = pl.ds(pl.multiple_of(c * CHUNK, CHUNK), CHUNK)
        right = jnp.concatenate([d[:, cols] for d in dirs], axis=0)
        for b in range(ND - 1):
            dots = nn(left_ref[b * ROWS : (b + 1) * ROWS, :], right)
            vh, vl = feature_values(dots, waves, cols)
            high[(b + 1) * ROWS : (b + 2) * ROWS, cols] = vh
            low[(b + 1) * ROWS : (b + 2) * ROWS, cols] = vl
        return carry

    lax.fori_loop(0, width // CHUNK, step, 0, unroll=2)


def spread_kernel(parts, near, cores, high, low, *refs):
    outs, (tally, wide) = refs[:parts], refs[parts:]
    width = high.shape[1]
    n_rows = near.shape[1]
    tail = jnp.zeros((8, ROWS), F32)
    for slot in range(ND):
        ref = (cores if slot % 2 else near).at[slot // 2]
        cols = pl.ds(slot * ROWS, ROWS)
        tail = tail + ref[n_rows - 8 : n_rows, :]
        for part in range(parts):
            qh, ql = split(ref[part * C : (part + 1) * C, :])
            wide[part * C : (part + 1) * C, cols] = qh
            wide[(parts + part) * C : (parts + part + 1) * C, cols] = ql
    tally[...] = tail
    count = parts * C

    def chunk(c, carry):
        cols = pl.ds(pl.multiple_of(c * CHUNK, CHUNK), CHUNK)
        both = nn(wide[...], high[:, cols])
        cross = nn(wide[:count, :], low[:, cols])
        result = both[:count] + (both[count:] + cross)
        for part in range(parts):
            outs[part][:, cols] = result[part * C : (part + 1) * C]
        return carry

    lax.fori_loop(0, width // CHUNK, chunk, 0, unroll=True)


def step_kernel(k, last, *refs):
    it = iter(refs)
    take = lambda n: [next(it) for _ in range(n)]
    feat_in = take(4)
    own, tally, facts = take(3)
    spread = take(1 if k == 1 else 2)
    if not last:
        oh, ol, inv_h, inv_l = take(4)
    if k == 1:
        prox_prev, = take(1)
    else:
        z_prev, v_prev, e_prev, small = take(4)
    if last:
        out_m, out_z = take(2)
    else:
        z_out, v_out, e_out, small_out, send = take(5)
    width = spread[0].shape[1]
    n_rows = own.shape[0]

    def feat_total(rows):
        return (feat_in[0][rows, :] + feat_in[1][rows, :]) + (feat_in[2][rows, :] + feat_in[3][rows, :])

    feat_scalars = feat_total(pl.ds(n_rows - 8, 8))[0:1, :]
    doc_scalars = tally[0:1, :]
    first = pl.ds(0, C)
    second = pl.ds(C, C)
    at = lambda row, n: row[:, n : n + 1]
    if k == 1:
        rho = jnp.ones((1, 1), F32)
        inv_g = None
        quad = at(doc_scalars, 2)
    else:
        rho_prev = small[7 * C : 7 * C + 1, 0:1]
        primal = at(feat_scalars, 0) + at(doc_scalars, 5)
        dual = rho_prev * rho_prev * (ND * at(feat_scalars, 1) + at(doc_scalars, 6))
        g = jnp.sqrt(jnp.sqrt((primal + ratio_floor) / (dual + ratio_floor)))
        rho = rho_prev * g
        inv_g = 1.0 / g
        quad = at(doc_scalars, 2) + inv_g * (at(doc_scalars, 3) + inv_g * at(doc_scalars, 4))

    limit = shrink_level / (rho * ND)

    def chunk(c, carry):
        az, norm_p, norm_d = carry
        cols = pl.ds(pl.multiple_of(c * CHUNK, CHUNK), CHUNK)
        if k == 1:
            v = qsum = spread[0][:, cols]
            target = v * (1.0 / ND)
            z = target - jnp.clip(target, -limit, limit)
            e = -z
            p = e
        else:
            qsum = spread[0][:, cols] + spread[1][:, cols] * inv_g
            v = qsum + v_prev[:, cols] * inv_g
            z_old = z_prev[:, cols]
            target = z_old + v * (1.0 / ND)
            z = target - jnp.clip(target, -limit, limit)
            e = z_old - z
            p = e - e_prev[:, cols] * inv_g
        if last:
            out_z[cols, :] = (z * float(NF)).T
            return carry
        v_out[:, cols] = v
        z_out[:, cols] = z
        e_out[:, cols] = e
        norm_p = norm_p + jnp.sum(p * (ND * p + 2.0 * qsum), axis=0, keepdims=True)
        norm_d = norm_d + jnp.sum(e * e, axis=0, keepdims=True)
        zh, zl = split(z)
        az2 = nt(jnp.concatenate([zh, zl], axis=0), oh[0:ROWS, cols])
        az = az + ((az2[:C] + az2[C:]) + nt(zh, ol[0:ROWS, cols]))
        return az, norm_p, norm_d

    init = (jnp.zeros((C, ROWS), F32), jnp.zeros((1, CHUNK), F32), jnp.zeros((1, CHUNK), F32))
    az, norm_p, norm_d = lax.fori_loop(0, width // CHUNK, chunk, init, unroll=True)

    signs = facts[0:C, :]
    ratio = facts[C : 2 * C, :] / rho
    w_sum = feat_total(first)
    if k == 1:
        m_prev = prox_prev[...]
    else:
        m_prev = small[0:C, :]
        w_sum = w_sum + (feat_total(second) + small[C : 2 * C, :]) * inv_g
    target = m_prev - w_sum
    margins = logistic_prox(target, signs, ratio)
    if last:
        out_m[...] = margins.T
        return
    if k == 1:
        b_prev = jnp.zeros((C, ROWS), F32)
        w = own[first, :]
        y = m_prev * (1.0 / NF) - w
        az_prev = jnp.zeros((C, ROWS), F32)
    else:
        b_prev = small[2 * C : 3 * C, :] * inv_g
        w = own[first, :] + (own[second, :] + small[3 * C : 4 * C, :]) * inv_g
        y = small[4 * C : 5 * C, :] + (m_prev - b_prev - small[5 * C : 6 * C, :]) * (1.0 / NF) - w
        az_prev = small[6 * C : 7 * C, :]
    b_new = target - margins
    sums = target - b_prev
    small_out[0:C, :] = margins
    small_out[C : 2 * C, :] = w_sum
    small_out[2 * C : 3 * C, :] = b_new
    small_out[3 * C : 4 * C, :] = w
    small_out[4 * C : 5 * C, :] = y
    small_out[5 * C : 6 * C, :] = sums
    small_out[6 * C : 7 * C, :] = az
    small_out[7 * C : 7 * C + 8, :] = jnp.broadcast_to(rho, (8, 128))
    ru = y + (margins - sums) * (1.0 / NF) - az
    rv = az_prev - az - w - b_new * (1.0 / NF)
    rh, rl = split(jnp.concatenate([ru, rv], axis=0))
    ih = inv_h[...]
    solved = nn(rh, ih) + (nn(rl, ih) + nn(rh, inv_l[...]))
    u = solved[:C]
    v2 = solved[C:]
    send[0:C, :] = u
    send[C : 2 * C, :] = v2
    part = rv - v2
    gap = sums - margins
    move = margins - m_prev
    send[2 * C : 2 * C + 8, :] = pack(
        [
            jnp.sum(norm_p, axis=1, keepdims=True) + quad,
            jnp.sum(norm_d, axis=1, keepdims=True),
            total(u * (ru - u)),
            2.0 * total(u * part),
            total(v2 * part),
            total(gap * gap),
            total(move * move),
        ]
    )


def table(move):
    pairs = []
    for d in range(ND):
        for f in range(NF):
            z, core, x, y = d // 2, d % 2, f // 4, f % 4
            z2, core2, x2, y2 = move(z, core, x, y)
            pairs.append((d * NF + f, ((z2 % 4) * 2 + core2) * NF + (x2 % 4) * 4 + y2 % 4))
    return pairs


def along_y(v, k):
    return lax.ppermute(v, AXES, table(lambda z, c, x, y: (z, c, x, y + k)))


def along_x(v, k):
    return lax.ppermute(v, AXES, table(lambda z, c, x, y: (z, c, x + k, y)))


def along_z(v, k):
    return lax.ppermute(v, AXES, table(lambda z, c, x, y: (z + k, c, x, y)))


def across(v):
    return lax.ppermute(v, AXES, table(lambda z, c, x, y: (z, 1 - c, x, y)))


def call(body, outs, scratch=(), flops=0, limit=24):
    return pl.pallas_call(
        body,
        out_shape=outs,
        scratch_shapes=list(scratch),
        cost_estimate=pl.CostEstimate(flops=flops, bytes_accessed=0, transcendentals=0),
        compiler_params=pltpu.CompilerParams(vmem_limit_bytes=limit * 1024 * 1024),
    )


def shape(*dims, dtype=F32):
    return jax.ShapeDtypeStruct(dims, dtype)


def gather_line(v, move):
    return [v] + [move(v, k) for k in (1, 2, 3)]


def per_device(documents, directions, phase, amplitude, doc_weight, labels):
    width = directions.shape[1]
    dirs = gather_line(directions, along_z)
    docs = lax.all_to_all(
        jnp.broadcast_to(documents.T[None], (NF,) + documents.T.shape), "feat", 0, 0
    )
    waves, facts, prox, copied = call(
        prepare_kernel,
        [
            shape(8, width),
            shape(2 * C, ROWS),
            shape(C, ROWS),
            shape(*directions.shape, dtype=BF16),
        ],
    )(
        phase.reshape(1, width),
        amplitude.reshape(1, width),
        labels.reshape(1, ROWS),
        doc_weight.reshape(1, ROWS),
        directions,
    )
    dirs[0] = copied
    dirs, docs, waves, facts, prox = lax.optimization_barrier((dirs, docs, waves, facts, prox))
    dirs_other = [across(d) for d in dirs]
    docs = docs.reshape(-1, ROWS)
    all_dirs = dirs + dirs_other
    high, low, inv_h, inv_l, send = call(
        own_kernel,
        [
            shape(ROWS, width, dtype=BF16),
            shape(ROWS, width, dtype=BF16),
            shape(ROWS, ROWS, dtype=BF16),
            shape(ROWS, ROWS, dtype=BF16),
            shape(C + 8, ROWS),
        ],
    )(docs, waves, prox, *all_dirs)

    docs_z, send = lax.optimization_barrier((gather_line(docs, along_z), send))
    docs_z = jnp.stack(docs_z)
    docs_c = across(docs_z)
    every = ND * ROWS
    high, low = call(
        other_kernel,
        [shape(every, width, dtype=BF16), shape(every, width, dtype=BF16)],
        [pltpu.VMEM((every - ROWS, docs.shape[0]), BF16)],
        flops=10**10,
    )(docs_z, docs_c, high, low, waves, *all_dirs)

    state = [prox]
    for k in range(1, ITERS + 1):
        last = k == ITERS
        parts = 1 if k == 1 else 2
        if last:
            outs = [shape(ROWS, C), shape(width, C)]
            mats = []
        else:
            outs = [
                shape(C, width),
                shape(C, width),
                shape(C, width),
                shape(7 * C + 8, ROWS),
                shape(2 * C + 8, ROWS),
            ]
            mats = [high, low, inv_h, inv_l]
        zs = gather_line(send, along_z)
        ys = gather_line(send, along_y)
        if k == 1:
            zs, ys, high, low = lax.optimization_barrier((zs, ys, high, low))
        else:
            ys = lax.optimization_barrier(ys)
        line = (ys[0] + ys[1]) + (ys[2] + ys[3])
        zs, _ = lax.optimization_barrier((zs, line))
        near = jnp.stack(zs)
        cores = across(near)
        xs = gather_line(line, along_x)
        *spread, tally = call(
            functools.partial(spread_kernel, parts),
            [shape(C, width)] * parts + [shape(8, ROWS)],
            [pltpu.VMEM((2 * parts * C, ND * ROWS), BF16)],
            flops=0,
        )(near, cores, high, low)
        out = call(functools.partial(step_kernel, k, last), outs)(
            *xs, send, tally, facts, *spread, *mats, *state
        )
        if not last:
            *state, send = out
    return tuple(out)


def solution(mesh):
    in_specs = (P("doc", "feat"), P("doc", "feat"), P("feat"), P("feat"), P("doc"), P("doc"))
    out_specs = (P("doc", None), P("feat", None))
    return jax.shard_map(
        per_device, mesh=mesh, in_specs=in_specs, out_specs=out_specs, check_vma=False
    )
```

```python
import functools

import jax
import jax.numpy as jnp
from jax import lax
from jax.experimental import pallas as pl
from jax.experimental.pallas import tpu as pltpu
from jax.sharding import PartitionSpec as P

C = 128
ITERS = 3
NEWTON = 3
ND = 8
NF = 16
ROWS = 128
CHUNK = 256

shrink_level = 0.1
ratio_floor = 1e-06

AXES = ("doc", "feat")
F32 = jnp.float32
BF16 = jnp.bfloat16
SIN_TERMS = (
    0.07765547442052619,
    -0.5982903290573769,
    2.5500773950715985,
    -5.1677100781672785,
    3.1415926400973193,
)
INV_TWO_PI = 0.15915494309189535


def nn(a, b):
    return lax.dot_general(a, b, (((1,), (0,)), ((), ())), preferred_element_type=F32)


def nt(a, b):
    return lax.dot_general(a, b, (((1,), (1,)), ((), ())), preferred_element_type=F32)


def split(v):
    high = v.astype(BF16)
    return high, (v - high.astype(F32)).astype(BF16)


def product(a, b, dot=nn):
    ah, al = split(a)
    bh, bl = split(b)
    return dot(ah, bh) + (dot(ah, bl) + dot(al, bh))


def split3(v):
    high = v.astype(BF16)
    rest = v - high.astype(F32)
    mid = rest.astype(BF16)
    return high, mid, (rest - mid.astype(F32)).astype(BF16)


def full_product(a, b):
    ah, am, al = split3(a)
    bh, bm, bl = split3(b)
    small = nn(am, bm) + (nn(ah, bl) + nn(al, bh))
    return nn(ah, bh) + ((nn(ah, bm) + nn(am, bh)) + small)


def feature_values(dots, waves, cols):
    turns = dots * INV_TWO_PI + waves[0:1, cols]
    part = turns - jnp.round(turns)
    square = part * part
    series = SIN_TERMS[0]
    for term in SIN_TERMS[1:]:
        series = series * square + term
    sine = series * part
    return split(waves[1:2, cols] - waves[2:3, cols] * (sine * sine))


def logistic_prox(target, signs, weight_ratio):
    current = target
    for _ in range(NEWTON):
        chance = 1.0 / (1.0 + jnp.exp(signs * current))
        gradient = current - target - weight_ratio * signs * chance
        current = current - gradient / (1.0 + weight_ratio * chance * (1.0 - chance))
    return current


def signs_of(labels_ref):
    labels = labels_ref[...]
    classes = lax.broadcasted_iota(jnp.int32, (C, ROWS), 0)
    return jnp.where(jnp.broadcast_to(labels, (C, ROWS)) == classes, 1.0, -1.0).astype(F32)


def total(v):
    return jnp.sum(jnp.sum(v, axis=0, keepdims=True), axis=1, keepdims=True)


def pack(values):
    lane = lax.broadcasted_iota(jnp.int32, (8, 128), 1)
    out = jnp.zeros((8, 128), F32)
    for k, v in enumerate(values):
        if v is not None:
            out = jnp.where(lane == k, jnp.broadcast_to(v, (8, 128)), out)
    return out


def inverse(matrix):
    n = matrix.shape[0]
    row_id = lax.broadcasted_iota(jnp.int32, (n, n), 0)
    col_id = lax.broadcasted_iota(jnp.int32, (n, n), 1)
    unit = jnp.where(row_id == col_id, 1.0, 0.0)
    top = jnp.max(jnp.sum(jnp.abs(matrix), axis=0))
    alpha = 2.0 / (top + 1.0)
    residual = unit - matrix * alpha
    guess = unit * alpha
    shrink = (top - 1.0) * (0.5 * alpha)

    def wide(carry):
        return carry[2] > 1e-4

    def double(carry):
        x, r, rate = carry
        rh, rl = split(r)
        xh, xl = split(x)
        both = nn(jnp.concatenate([xh, rh, xl, rl], axis=0), rh)
        cross = nn(jnp.concatenate([xh, rh], axis=0), rl)
        both = both[: 2 * n] + (both[2 * n :] + cross)
        return x + both[:n], both[n:], rate * rate

    guess, _, _ = lax.while_loop(wide, double, (guess, residual, shrink))

    def inexact(carry):
        return carry[1] > 1e-3

    def correct(carry):
        x, _ = carry
        r = unit - full_product(matrix, x)
        size = jnp.max(jnp.sum(jnp.abs(r), axis=0))
        return x + product(x, r), size

    guess, _ = lax.while_loop(inexact, correct, (guess, jnp.float32(1.0)))
    return guess


def doc_piece(docs_ref, slot):
    place = lax.axis_index("doc")
    block = ((place // 2 - slot // 2 + 4) % 4) * 2 + (place % 2 + slot % 2) % 2
    feat = lax.axis_index("feat")
    rows = docs_ref.shape[0] // NF
    pieces = []
    for half in range(2):
        source = 2 * block + half
        spot = source
        pieces.append(docs_ref[pl.ds(pl.multiple_of(rows * spot, rows), rows), :])
    return jnp.concatenate(pieces, axis=0)


def prepare_kernel(phase, amp, labels, weight, dirs, waves, facts, prox_ref, copied):
    copied[...] = dirs[...]
    width = phase.shape[1]
    scale = amp[...] * (2.0 / width) ** 0.5
    waves[0:1, :] = phase[...] * INV_TWO_PI
    waves[1:2, :] = scale
    waves[2:3, :] = scale + scale
    signs = signs_of(labels)
    wide = jnp.broadcast_to(weight[...], (C, ROWS))
    facts[0:C, :] = signs
    facts[C : 2 * C, :] = wide
    prox_ref[...] = logistic_prox(jnp.zeros((C, ROWS), F32), signs, wide)


def own_kernel(docs, waves, prox, d0, d1, d2, d3, e0, e1, e2, e3, high, low, inv_h, inv_l, send):
    dirs = (d0, e0, d1, e1, d2, e2, d3, e3)
    left = jnp.concatenate([doc_piece(docs, s) for s in range(ND)], axis=0)
    left = left.astype(F32).T.astype(BF16)
    width = waves.shape[1]
    gram = jnp.zeros((ROWS, 2 * ROWS), F32)
    for start in range(0, width, CHUNK):
        cols = pl.ds(start, CHUNK)
        right = jnp.concatenate([d[:, cols] for d in dirs], axis=0)
        vh, vl = feature_values(nn(left, right), waves, cols)
        high[:, cols] = vh
        low[:, cols] = vl
        gram = gram + nt(vh, jnp.concatenate([vh, vl], axis=0))
    cross = gram[:, ROWS:]
    row_id = lax.broadcasted_iota(jnp.int32, (ROWS, ROWS), 0)
    col_id = lax.broadcasted_iota(jnp.int32, (ROWS, ROWS), 1)
    whole = gram[:, :ROWS] + (cross + cross.T) + jnp.where(row_id == col_id, 1.0, 0.0)
    inv = inverse(whole)
    ih, il = split(inv)
    inv_h[...] = ih
    inv_l[...] = il
    right_side = prox[...] * (1.0 / NF)
    w = product(right_side, inv)
    send[0:C, :] = w
    send[C : C + 8, :] = pack([None, None, total(w * (right_side - w))])


def fill_blocks(left_ref, blocks, dirs, waves, high, low, first):
    width = waves.shape[1]
    for b, block in enumerate(blocks):
        left = jnp.concatenate([doc_piece(block, s) for s in range(ND)], axis=0)
        left_ref[b * ROWS : (b + 1) * ROWS, :] = left.astype(F32).T.astype(BF16)

    def step(c, carry):
        cols = pl.ds(pl.multiple_of(c * CHUNK, CHUNK), CHUNK)
        right = jnp.concatenate([d[:, cols] for d in dirs], axis=0)
        for b in range(len(blocks)):
            dots = nn(left_ref[b * ROWS : (b + 1) * ROWS, :], right)
            vh, vl = feature_values(dots, waves, cols)
            high[(first + b) * ROWS : (first + b + 1) * ROWS, cols] = vh
            low[(first + b) * ROWS : (first + b + 1) * ROWS, cols] = vl
        return carry

    lax.fori_loop(0, width // CHUNK, step, 0, unroll=2)


def near_kernel(docs_1, docs_2, docs_3, own_h, own_l, waves, d0, d1, d2, d3, e0, e1, e2, e3, high, low, left_ref):
    high[0:ROWS, :] = own_h[...]
    low[0:ROWS, :] = own_l[...]
    dirs = (d0, e0, d1, e1, d2, e2, d3, e3)
    fill_blocks(left_ref, [docs_1, docs_2, docs_3], dirs, waves, high, low, 1)


def far_kernel(docs, waves, d0, d1, d2, d3, e0, e1, e2, e3, high, low, left_ref):
    dirs = (d0, e0, d1, e1, d2, e2, d3, e3)
    fill_blocks(left_ref, [docs.at[b] for b in range(4)], dirs, waves, high, low, 0)


def spread_kernel(parts, *refs):
    near, refs = refs[:4], refs[4:]
    far, mats, refs = refs[0], refs[1:5], refs[5:]
    outs, wide = refs[:parts], refs[parts]
    width = mats[0].shape[1]
    n_rows = near[0].shape[0]
    blocks = list(near) + [far.at[b] for b in range(4)]
    tail = jnp.zeros((8, ROWS), F32)
    for slot, ref in enumerate(blocks):
        cols = pl.ds(slot * ROWS, ROWS)
        tail = tail + ref[n_rows - 8 : n_rows, :]
        for part in range(parts):
            qh, ql = split(ref[part * C : (part + 1) * C, :])
            wide[part * C : (part + 1) * C, cols] = qh
            wide[(parts + part) * C : (parts + part + 1) * C, cols] = ql
    outs[0][C : C + 8, 0:ROWS] = tail
    count = parts * C
    depth = 4 * ROWS

    def chunk(c, carry):
        cols = pl.ds(pl.multiple_of(c * CHUNK, CHUNK), CHUNK)
        both = nn(wide[:, :depth], mats[0][:, cols]) + nn(wide[:, depth:], mats[2][:, cols])
        cross = nn(wide[:count, :depth], mats[1][:, cols]) + nn(wide[:count, depth:], mats[3][:, cols])
        result = both[:count] + (both[count:] + cross)
        for part in range(parts):
            outs[part][0:C, cols] = result[part * C : (part + 1) * C]
        return carry

    lax.fori_loop(0, width // CHUNK, chunk, 0, unroll=True)


def step_kernel(k, last, *refs):
    it = iter(refs)
    take = lambda n: [next(it) for _ in range(n)]
    feat_in = take(4)
    own, facts = take(2)
    spread = take(1 if k == 1 else 2)
    if not last:
        oh, ol, inv_h, inv_l = take(4)
    if k == 1:
        prox_prev, = take(1)
    else:
        z_prev, v_prev, e_prev, small = take(4)
    if last:
        out_m, out_z = take(2)
    else:
        z_out, v_out, e_out, small_out, send = take(5)
    width = spread[0].shape[1]
    n_rows = own.shape[0]

    def feat_total(rows):
        return (feat_in[0][rows, :] + feat_in[1][rows, :]) + (feat_in[2][rows, :] + feat_in[3][rows, :])

    feat_scalars = feat_total(pl.ds(n_rows - 8, 8))[0:1, :]
    doc_scalars = spread[0][C : C + 1, 0:ROWS]
    first = pl.ds(0, C)
    second = pl.ds(C, C)
    at = lambda row, n: row[:, n : n + 1]
    if k == 1:
        rho = jnp.ones((1, 1), F32)
        inv_g = None
        quad = at(doc_scalars, 2)
    else:
        rho_prev = small[7 * C : 7 * C + 1, 0:1]
        primal = at(feat_scalars, 0) + at(doc_scalars, 5)
        dual = rho_prev * rho_prev * (ND * at(feat_scalars, 1) + at(doc_scalars, 6))
        g = jnp.sqrt(jnp.sqrt((primal + ratio_floor) / (dual + ratio_floor)))
        rho = rho_prev * g
        inv_g = 1.0 / g
        quad = at(doc_scalars, 2) + inv_g * (at(doc_scalars, 3) + inv_g * at(doc_scalars, 4))

    limit = shrink_level / (rho * ND)

    def chunk(c, carry):
        az, norm_p, norm_d = carry
        cols = pl.ds(pl.multiple_of(c * CHUNK, CHUNK), CHUNK)
        if k == 1:
            v = qsum = spread[0][0:C, cols]
            target = v * (1.0 / ND)
            z = target - jnp.clip(target, -limit, limit)
            e = -z
            p = e
        else:
            qsum = spread[0][0:C, cols] + spread[1][0:C, cols] * inv_g
            v = qsum + v_prev[:, cols] * inv_g
            z_old = z_prev[:, cols]
            target = z_old + v * (1.0 / ND)
            z = target - jnp.clip(target, -limit, limit)
            e = z_old - z
            p = e - e_prev[:, cols] * inv_g
        if last:
            out_z[cols, :] = (z * float(NF)).T
            return carry
        v_out[:, cols] = v
        z_out[:, cols] = z
        e_out[:, cols] = e
        norm_p = norm_p + jnp.sum(p * (ND * p + 2.0 * qsum), axis=0, keepdims=True)
        norm_d = norm_d + jnp.sum(e * e, axis=0, keepdims=True)
        zh, zl = split(z)
        az2 = nt(jnp.concatenate([zh, zl], axis=0), oh[0:ROWS, cols])
        az = az + ((az2[:C] + az2[C:]) + nt(zh, ol[0:ROWS, cols]))
        return az, norm_p, norm_d

    init = (jnp.zeros((C, ROWS), F32), jnp.zeros((1, CHUNK), F32), jnp.zeros((1, CHUNK), F32))
    az, norm_p, norm_d = lax.fori_loop(0, width // CHUNK, chunk, init, unroll=True)

    signs = facts[0:C, :]
    ratio = facts[C : 2 * C, :] / rho
    w_sum = feat_total(first)
    if k == 1:
        m_prev = prox_prev[...]
    else:
        m_prev = small[0:C, :]
        w_sum = w_sum + (feat_total(second) + small[C : 2 * C, :]) * inv_g
    target = m_prev - w_sum
    margins = logistic_prox(target, signs, ratio)
    if last:
        out_m[...] = margins.T
        return
    if k == 1:
        b_prev = jnp.zeros((C, ROWS), F32)
        w = own[first, :]
        y = m_prev * (1.0 / NF) - w
        az_prev = jnp.zeros((C, ROWS), F32)
    else:
        b_prev = small[2 * C : 3 * C, :] * inv_g
        w = own[first, :] + (own[second, :] + small[3 * C : 4 * C, :]) * inv_g
        y = small[4 * C : 5 * C, :] + (m_prev - b_prev - small[5 * C : 6 * C, :]) * (1.0 / NF) - w
        az_prev = small[6 * C : 7 * C, :]
    b_new = target - margins
    sums = target - b_prev
    small_out[0:C, :] = margins
    small_out[C : 2 * C, :] = w_sum
    small_out[2 * C : 3 * C, :] = b_new
    small_out[3 * C : 4 * C, :] = w
    small_out[4 * C : 5 * C, :] = y
    small_out[5 * C : 6 * C, :] = sums
    small_out[6 * C : 7 * C, :] = az
    small_out[7 * C : 7 * C + 8, :] = jnp.broadcast_to(rho, (8, 128))
    ru = y + (margins - sums) * (1.0 / NF) - az
    rv = az_prev - az - w - b_new * (1.0 / NF)
    rh, rl = split(jnp.concatenate([ru, rv], axis=0))
    ih = inv_h[...]
    solved = nn(rh, ih) + (nn(rl, ih) + nn(rh, inv_l[...]))
    u = solved[:C]
    v2 = solved[C:]
    send[0:C, :] = u
    send[C : 2 * C, :] = v2
    part = rv - v2
    gap = sums - margins
    move = margins - m_prev
    send[2 * C : 2 * C + 8, :] = pack(
        [
            jnp.sum(norm_p, axis=1, keepdims=True) + quad,
            jnp.sum(norm_d, axis=1, keepdims=True),
            total(u * (ru - u)),
            2.0 * total(u * part),
            total(v2 * part),
            total(gap * gap),
            total(move * move),
        ]
    )


def table(move):
    pairs = []
    for d in range(ND):
        for f in range(NF):
            z, core, x, y = d // 2, d % 2, f // 4, f % 4
            z2, core2, x2, y2 = move(z, core, x, y)
            pairs.append((d * NF + f, ((z2 % 4) * 2 + core2) * NF + (x2 % 4) * 4 + y2 % 4))
    return pairs


def along_y(v, k):
    return lax.ppermute(v, AXES, table(lambda z, c, x, y: (z, c, x, y + k)))


def along_x(v, k):
    return lax.ppermute(v, AXES, table(lambda z, c, x, y: (z, c, x + k, y)))


def along_z(v, k):
    return lax.ppermute(v, AXES, table(lambda z, c, x, y: (z + k, c, x, y)))


def across(v):
    return lax.ppermute(v, AXES, table(lambda z, c, x, y: (z, 1 - c, x, y)))


def call(body, outs, scratch=(), flops=0, limit=24):
    return pl.pallas_call(
        body,
        out_shape=outs,
        scratch_shapes=list(scratch),
        cost_estimate=pl.CostEstimate(flops=flops, bytes_accessed=0, transcendentals=0),
        compiler_params=pltpu.CompilerParams(vmem_limit_bytes=limit * 1024 * 1024),
    )


def shape(*dims, dtype=F32):
    return jax.ShapeDtypeStruct(dims, dtype)


def gather_line(v, move):
    return [v] + [move(v, k) for k in (1, 2, 3)]


def per_device(documents, directions, phase, amplitude, doc_weight, labels):
    width = directions.shape[1]
    dirs = gather_line(directions, along_z)
    docs = lax.all_to_all(
        jnp.broadcast_to(documents.T[None], (NF,) + documents.T.shape), "feat", 0, 0
    )
    waves, facts, prox, copied = call(
        prepare_kernel,
        [
            shape(8, width),
            shape(2 * C, ROWS),
            shape(C, ROWS),
            shape(*directions.shape, dtype=BF16),
        ],
    )(
        phase.reshape(1, width),
        amplitude.reshape(1, width),
        labels.reshape(1, ROWS),
        doc_weight.reshape(1, ROWS),
        directions,
    )
    dirs[0] = copied
    dirs, docs, waves, facts, prox = lax.optimization_barrier((dirs, docs, waves, facts, prox))
    dirs_other = [across(d) for d in dirs]
    docs = docs.reshape(-1, ROWS)
    all_dirs = dirs + dirs_other
    high, low, inv_h, inv_l, send = call(
        own_kernel,
        [
            shape(ROWS, width, dtype=BF16),
            shape(ROWS, width, dtype=BF16),
            shape(ROWS, ROWS, dtype=BF16),
            shape(ROWS, ROWS, dtype=BF16),
            shape(C + 8, ROWS),
        ],
    )(docs, waves, prox, *all_dirs)

    docs_z, _ = lax.optimization_barrier((gather_line(docs, along_z), send))
    quarter = [shape(4 * ROWS, width, dtype=BF16), shape(4 * ROWS, width, dtype=BF16)]
    near_h, near_l = call(
        near_kernel, quarter, [pltpu.VMEM((3 * ROWS, docs.shape[0]), BF16)], flops=10**7
    )(*docs_z[1:], high, low, waves, *all_dirs)

    state = [prox]
    for k in range(1, ITERS + 1):
        last = k == ITERS
        parts = 1 if k == 1 else 2
        if last:
            outs = [shape(ROWS, C), shape(width, C)]
            mats = []
        else:
            outs = [
                shape(C, width),
                shape(C, width),
                shape(C, width),
                shape(7 * C + 8, ROWS),
                shape(2 * C + 8, ROWS),
            ]
            mats = [near_h, near_l, inv_h, inv_l]
        zs = gather_line(send, along_z)
        ys = gather_line(send, along_y)
        if k == 1:
            zs, ys, near_h, near_l = lax.optimization_barrier((zs, ys, near_h, near_l))
        else:
            ys = lax.optimization_barrier(ys)
        line = (ys[0] + ys[1]) + (ys[2] + ys[3])
        if k > 1:
            zs, _ = lax.optimization_barrier((zs, line))
        xs = gather_line(line, along_x)
        if k == 1:
            docs_z, _ = lax.optimization_barrier((docs_z, line))
            far_h, far_l = call(
                far_kernel, quarter, [pltpu.VMEM((4 * ROWS, docs.shape[0]), BF16)], flops=10**10
            )(across(jnp.stack(docs_z)), waves, *all_dirs)
        spread = call(
            functools.partial(spread_kernel, parts),
            [shape(C + 8, width), shape(C, width)][:parts],
            [pltpu.VMEM((2 * parts * C, ND * ROWS), BF16)],
        )(*zs, across(jnp.stack(zs)), near_h, near_l, far_h, far_l)
        out = call(functools.partial(step_kernel, k, last), outs)(
            *xs, send, facts, *spread, *mats, *state
        )
        if not last:
            *state, send = out
    return tuple(out)


def solution(mesh):
    in_specs = (P("doc", "feat"), P("doc", "feat"), P("feat"), P("feat"), P("doc"), P("doc"))
    out_specs = (P("doc", None), P("feat", None))
    return jax.shard_map(
        per_device, mesh=mesh, in_specs=in_specs, out_specs=out_specs, check_vma=False
    )
```

```python
import functools

import jax
import jax.numpy as jnp
from jax import lax
from jax.experimental import pallas as pl
from jax.experimental.pallas import tpu as pltpu
from jax.sharding import PartitionSpec as P

C = 128
ITERS = 3
NEWTON = 3
ND = 8
NF = 16
ROWS = 128
CHUNK = 256

shrink_level = 0.1
ratio_floor = 1e-06

AXES = ("doc", "feat")
F32 = jnp.float32
BF16 = jnp.bfloat16
SIN_TERMS = (
    0.07765547442052619,
    -0.5982903290573769,
    2.5500773950715985,
    -5.1677100781672785,
    3.1415926400973193,
)
INV_TWO_PI = 0.15915494309189535


def nn(a, b):
    return lax.dot_general(a, b, (((1,), (0,)), ((), ())), preferred_element_type=F32)


def nt(a, b):
    return lax.dot_general(a, b, (((1,), (1,)), ((), ())), preferred_element_type=F32)


def split(v):
    high = v.astype(BF16)
    return high, (v - high.astype(F32)).astype(BF16)


def product(a, b, dot=nn):
    ah, al = split(a)
    bh, bl = split(b)
    return dot(ah, bh) + (dot(ah, bl) + dot(al, bh))


def split3(v):
    high = v.astype(BF16)
    rest = v - high.astype(F32)
    mid = rest.astype(BF16)
    return high, mid, (rest - mid.astype(F32)).astype(BF16)


def full_product(a, b):
    ah, am, al = split3(a)
    bh, bm, bl = split3(b)
    small = nn(am, bm) + (nn(ah, bl) + nn(al, bh))
    return nn(ah, bh) + ((nn(ah, bm) + nn(am, bh)) + small)


def feature_values(dots, waves, cols):
    turns = dots * INV_TWO_PI + waves[0:1, cols]
    part = turns - jnp.round(turns)
    square = part * part
    series = SIN_TERMS[0]
    for term in SIN_TERMS[1:]:
        series = series * square + term
    sine = series * part
    return split(waves[1:2, cols] - waves[2:3, cols] * (sine * sine))


def logistic_prox(target, signs, weight_ratio):
    current = target
    for _ in range(NEWTON):
        chance = 1.0 / (1.0 + jnp.exp(signs * current))
        gradient = current - target - weight_ratio * signs * chance
        current = current - gradient / (1.0 + weight_ratio * chance * (1.0 - chance))
    return current


def signs_of(labels_ref):
    labels = labels_ref[...]
    classes = lax.broadcasted_iota(jnp.int32, (C, ROWS), 0)
    return jnp.where(jnp.broadcast_to(labels, (C, ROWS)) == classes, 1.0, -1.0).astype(F32)


def total(v):
    return jnp.sum(jnp.sum(v, axis=0, keepdims=True), axis=1, keepdims=True)


def pack(values):
    lane = lax.broadcasted_iota(jnp.int32, (8, 128), 1)
    out = jnp.zeros((8, 128), F32)
    for k, v in enumerate(values):
        if v is not None:
            out = jnp.where(lane == k, jnp.broadcast_to(v, (8, 128)), out)
    return out


def inverse(matrix):
    n = matrix.shape[0]
    row_id = lax.broadcasted_iota(jnp.int32, (n, n), 0)
    col_id = lax.broadcasted_iota(jnp.int32, (n, n), 1)
    unit = jnp.where(row_id == col_id, 1.0, 0.0)
    top = jnp.max(jnp.sum(jnp.abs(matrix), axis=0))
    alpha = 2.0 / (top + 1.0)
    residual = unit - matrix * alpha
    guess = unit * alpha
    shrink = (top - 1.0) * (0.5 * alpha)

    def wide(carry):
        return carry[2] > 1e-4

    def double(carry):
        x, r, rate = carry
        rh, rl = split(r)
        xh, xl = split(x)
        both = nn(jnp.concatenate([xh, rh, xl, rl], axis=0), rh)
        cross = nn(jnp.concatenate([xh, rh], axis=0), rl)
        both = both[: 2 * n] + (both[2 * n :] + cross)
        return x + both[:n], both[n:], rate * rate

    guess, _, _ = lax.while_loop(wide, double, (guess, residual, shrink))

    def inexact(carry):
        return jnp.logical_and(carry[1] > 1e-3, carry[2] < 6)

    def correct(carry):
        x, _, count = carry
        r = unit - full_product(matrix, x)
        size = jnp.max(jnp.sum(jnp.abs(r), axis=0))
        return x + product(x, r), size, count + 1

    start = (guess, jnp.float32(1.0), jnp.int32(0))
    guess, _, _ = lax.while_loop(inexact, correct, start)
    return guess


def doc_piece(docs_ref, slot):
    place = lax.axis_index("doc")
    block = ((place // 2 - slot // 2 + 4) % 4) * 2 + (place % 2 + slot % 2) % 2
    feat = lax.axis_index("feat")
    rows = docs_ref.shape[0] // NF
    pieces = []
    for half in range(2):
        source = 2 * block + half
        spot = source
        pieces.append(docs_ref[pl.ds(pl.multiple_of(rows * spot, rows), rows), :])
    return jnp.concatenate(pieces, axis=0)


def prepare_kernel(phase, amp, labels, weight, dirs, waves, facts, prox_ref, copied):
    copied[...] = dirs[...]
    width = phase.shape[1]
    scale = amp[...] * (2.0 / width) ** 0.5
    waves[0:1, :] = phase[...] * INV_TWO_PI
    waves[1:2, :] = scale
    waves[2:3, :] = scale + scale
    signs = signs_of(labels)
    wide = jnp.broadcast_to(weight[...], (C, ROWS))
    facts[0:C, :] = signs
    facts[C : 2 * C, :] = wide
    prox_ref[...] = logistic_prox(jnp.zeros((C, ROWS), F32), signs, wide)


def own_kernel(docs, waves, prox, d0, d1, d2, d3, e0, e1, e2, e3, high, low, inv_h, inv_l, send):
    dirs = (d0, e0, d1, e1, d2, e2, d3, e3)
    left = jnp.concatenate([doc_piece(docs, s) for s in range(ND)], axis=0)
    left = left.astype(F32).T.astype(BF16)
    width = waves.shape[1]
    gram = jnp.zeros((ROWS, 2 * ROWS), F32)
    for start in range(0, width, CHUNK):
        cols = pl.ds(start, CHUNK)
        right = jnp.concatenate([d[:, cols] for d in dirs], axis=0)
        vh, vl = feature_values(nn(left, right), waves, cols)
        high[:, cols] = vh
        low[:, cols] = vl
        gram = gram + nt(vh, jnp.concatenate([vh, vl], axis=0))
    cross = gram[:, ROWS:]
    row_id = lax.broadcasted_iota(jnp.int32, (ROWS, ROWS), 0)
    col_id = lax.broadcasted_iota(jnp.int32, (ROWS, ROWS), 1)
    whole = gram[:, :ROWS] + (cross + cross.T) + jnp.where(row_id == col_id, 1.0, 0.0)
    inv = inverse(whole)
    ih, il = split(inv)
    inv_h[...] = ih
    inv_l[...] = il
    right_side = prox[...] * (1.0 / NF)
    w = product(right_side, inv)
    send[0:C, :] = w
    send[C : C + 8, :] = pack([None, None, total(w * (right_side - w))])


def fill_blocks(left_ref, blocks, dirs, waves, high, low, first):
    width = waves.shape[1]
    for b, block in enumerate(blocks):
        left = jnp.concatenate([doc_piece(block, s) for s in range(ND)], axis=0)
        left_ref[b * ROWS : (b + 1) * ROWS, :] = left.astype(F32).T.astype(BF16)

    def step(c, carry):
        cols = pl.ds(pl.multiple_of(c * CHUNK, CHUNK), CHUNK)
        right = jnp.concatenate([d[:, cols] for d in dirs], axis=0)
        for b in range(len(blocks)):
            dots = nn(left_ref[b * ROWS : (b + 1) * ROWS, :], right)
            vh, vl = feature_values(dots, waves, cols)
            high[(first + b) * ROWS : (first + b + 1) * ROWS, cols] = vh
            low[(first + b) * ROWS : (first + b + 1) * ROWS, cols] = vl
        return carry

    lax.fori_loop(0, width // CHUNK, step, 0, unroll=2)


def near_kernel(docs_1, docs_2, docs_3, own_h, own_l, waves, d0, d1, d2, d3, e0, e1, e2, e3, high, low, left_ref):
    high[0:ROWS, :] = own_h[...]
    low[0:ROWS, :] = own_l[...]
    dirs = (d0, e0, d1, e1, d2, e2, d3, e3)
    fill_blocks(left_ref, [docs_1, docs_2, docs_3], dirs, waves, high, low, 1)


def far_kernel(docs, waves, d0, d1, d2, d3, e0, e1, e2, e3, high, low, left_ref):
    dirs = (d0, e0, d1, e1, d2, e2, d3, e3)
    fill_blocks(left_ref, [docs.at[b] for b in range(4)], dirs, waves, high, low, 0)


def spread_kernel(parts, *refs):
    near, refs = refs[:4], refs[4:]
    far, mats, refs = refs[0], refs[1:5], refs[5:]
    outs, wide = refs[:parts], refs[parts]
    width = mats[0].shape[1]
    n_rows = near[0].shape[0]
    blocks = list(near) + [far.at[b] for b in range(4)]
    tail = jnp.zeros((8, ROWS), F32)
    for slot, ref in enumerate(blocks):
        cols = pl.ds(slot * ROWS, ROWS)
        tail = tail + ref[n_rows - 8 : n_rows, :]
        for part in range(parts):
            qh, ql = split(ref[part * C : (part + 1) * C, :])
            wide[part * C : (part + 1) * C, cols] = qh
            wide[(parts + part) * C : (parts + part + 1) * C, cols] = ql
    outs[0][C : C + 8, 0:ROWS] = tail
    count = parts * C
    depth = 4 * ROWS

    def chunk(c, carry):
        cols = pl.ds(pl.multiple_of(c * CHUNK, CHUNK), CHUNK)
        both = nn(wide[:, :depth], mats[0][:, cols]) + nn(wide[:, depth:], mats[2][:, cols])
        cross = nn(wide[:count, :depth], mats[1][:, cols]) + nn(wide[:count, depth:], mats[3][:, cols])
        result = both[:count] + (both[count:] + cross)
        for part in range(parts):
            outs[part][0:C, cols] = result[part * C : (part + 1) * C]
        return carry

    lax.fori_loop(0, width // CHUNK, chunk, 0, unroll=True)


def step_kernel(k, last, *refs):
    it = iter(refs)
    take = lambda n: [next(it) for _ in range(n)]
    feat_in = take(4)
    own, facts = take(2)
    spread = take(1 if k == 1 else 2)
    if not last:
        oh, ol, inv_h, inv_l = take(4)
    if k == 1:
        prox_prev, = take(1)
    else:
        z_prev, v_prev, e_prev, small = take(4)
    if last:
        out_m, out_z = take(2)
    else:
        z_out, v_out, e_out, small_out, send = take(5)
    width = spread[0].shape[1]
    n_rows = own.shape[0]

    def feat_total(rows):
        return (feat_in[0][rows, :] + feat_in[1][rows, :]) + (feat_in[2][rows, :] + feat_in[3][rows, :])

    feat_scalars = feat_total(pl.ds(n_rows - 8, 8))[0:1, :]
    doc_scalars = spread[0][C : C + 1, 0:ROWS]
    first = pl.ds(0, C)
    second = pl.ds(C, C)
    at = lambda row, n: row[:, n : n + 1]
    if k == 1:
        rho = jnp.ones((1, 1), F32)
        inv_g = None
        quad = at(doc_scalars, 2)
    else:
        rho_prev = small[7 * C : 7 * C + 1, 0:1]
        primal = at(feat_scalars, 0) + at(doc_scalars, 5)
        dual = rho_prev * rho_prev * (ND * at(feat_scalars, 1) + at(doc_scalars, 6))
        g = jnp.sqrt(jnp.sqrt((primal + ratio_floor) / (dual + ratio_floor)))
        rho = rho_prev * g
        inv_g = 1.0 / g
        quad = at(doc_scalars, 2) + inv_g * (at(doc_scalars, 3) + inv_g * at(doc_scalars, 4))

    limit = shrink_level / (rho * ND)

    def chunk(c, carry):
        az, norm_p, norm_d = carry
        cols = pl.ds(pl.multiple_of(c * CHUNK, CHUNK), CHUNK)
        if k == 1:
            v = qsum = spread[0][0:C, cols]
            target = v * (1.0 / ND)
            z = target - jnp.clip(target, -limit, limit)
            e = -z
            p = e
        else:
            qsum = spread[0][0:C, cols] + spread[1][0:C, cols] * inv_g
            v = qsum + v_prev[:, cols] * inv_g
            z_old = z_prev[:, cols]
            target = z_old + v * (1.0 / ND)
            z = target - jnp.clip(target, -limit, limit)
            e = z_old - z
            p = e - e_prev[:, cols] * inv_g
        if last:
            out_z[cols, :] = (z * float(NF)).T
            return carry
        v_out[:, cols] = v
        z_out[:, cols] = z
        e_out[:, cols] = e
        norm_p = norm_p + jnp.sum(p * (ND * p + 2.0 * qsum), axis=0, keepdims=True)
        norm_d = norm_d + jnp.sum(e * e, axis=0, keepdims=True)
        zh, zl = split(z)
        az2 = nt(jnp.concatenate([zh, zl], axis=0), oh[0:ROWS, cols])
        az = az + ((az2[:C] + az2[C:]) + nt(zh, ol[0:ROWS, cols]))
        return az, norm_p, norm_d

    init = (jnp.zeros((C, ROWS), F32), jnp.zeros((1, CHUNK), F32), jnp.zeros((1, CHUNK), F32))
    az, norm_p, norm_d = lax.fori_loop(0, width // CHUNK, chunk, init, unroll=True)

    signs = facts[0:C, :]
    ratio = facts[C : 2 * C, :] / rho
    w_sum = feat_total(first)
    if k == 1:
        m_prev = prox_prev[...]
    else:
        m_prev = small[0:C, :]
        w_sum = w_sum + (feat_total(second) + small[C : 2 * C, :]) * inv_g
    target = m_prev - w_sum
    margins = logistic_prox(target, signs, ratio)
    if last:
        out_m[...] = margins.T
        return
    if k == 1:
        b_prev = jnp.zeros((C, ROWS), F32)
        w = own[first, :]
        y = m_prev * (1.0 / NF) - w
        az_prev = jnp.zeros((C, ROWS), F32)
    else:
        b_prev = small[2 * C : 3 * C, :] * inv_g
        w = own[first, :] + (own[second, :] + small[3 * C : 4 * C, :]) * inv_g
        y = small[4 * C : 5 * C, :] + (m_prev - b_prev - small[5 * C : 6 * C, :]) * (1.0 / NF) - w
        az_prev = small[6 * C : 7 * C, :]
    b_new = target - margins
    sums = target - b_prev
    small_out[0:C, :] = margins
    small_out[C : 2 * C, :] = w_sum
    small_out[2 * C : 3 * C, :] = b_new
    small_out[3 * C : 4 * C, :] = w
    small_out[4 * C : 5 * C, :] = y
    small_out[5 * C : 6 * C, :] = sums
    small_out[6 * C : 7 * C, :] = az
    small_out[7 * C : 7 * C + 8, :] = jnp.broadcast_to(rho, (8, 128))
    ru = y + (margins - sums) * (1.0 / NF) - az
    rv = az_prev - az - w - b_new * (1.0 / NF)
    rh, rl = split(jnp.concatenate([ru, rv], axis=0))
    ih = inv_h[...]
    solved = nn(rh, ih) + (nn(rl, ih) + nn(rh, inv_l[...]))
    u = solved[:C]
    v2 = solved[C:]
    send[0:C, :] = u
    send[C : 2 * C, :] = v2
    part = rv - v2
    gap = sums - margins
    move = margins - m_prev
    send[2 * C : 2 * C + 8, :] = pack(
        [
            jnp.sum(norm_p, axis=1, keepdims=True) + quad,
            jnp.sum(norm_d, axis=1, keepdims=True),
            total(u * (ru - u)),
            2.0 * total(u * part),
            total(v2 * part),
            total(gap * gap),
            total(move * move),
        ]
    )


def table(move):
    pairs = []
    for d in range(ND):
        for f in range(NF):
            z, core, x, y = d // 2, d % 2, f // 4, f % 4
            z2, core2, x2, y2 = move(z, core, x, y)
            pairs.append((d * NF + f, ((z2 % 4) * 2 + core2) * NF + (x2 % 4) * 4 + y2 % 4))
    return pairs


def along_y(v, k):
    return lax.ppermute(v, AXES, table(lambda z, c, x, y: (z, c, x, y + k)))


def along_x(v, k):
    return lax.ppermute(v, AXES, table(lambda z, c, x, y: (z, c, x + k, y)))


def along_z(v, k):
    return lax.ppermute(v, AXES, table(lambda z, c, x, y: (z + k, c, x, y)))


def across(v):
    return lax.ppermute(v, AXES, table(lambda z, c, x, y: (z, 1 - c, x, y)))


def call(body, outs, scratch=(), flops=0, limit=24):
    return pl.pallas_call(
        body,
        out_shape=outs,
        scratch_shapes=list(scratch),
        cost_estimate=pl.CostEstimate(flops=flops, bytes_accessed=0, transcendentals=0),
        compiler_params=pltpu.CompilerParams(vmem_limit_bytes=limit * 1024 * 1024),
    )


def shape(*dims, dtype=F32):
    return jax.ShapeDtypeStruct(dims, dtype)


def gather_line(v, move):
    return [v] + [move(v, k) for k in (1, 2, 3)]


def per_device(documents, directions, phase, amplitude, doc_weight, labels):
    width = directions.shape[1]
    dirs = gather_line(directions, along_z)
    docs = lax.all_to_all(
        jnp.broadcast_to(documents.T[None], (NF,) + documents.T.shape), "feat", 0, 0
    )
    waves, facts, prox, copied = call(
        prepare_kernel,
        [
            shape(8, width),
            shape(2 * C, ROWS),
            shape(C, ROWS),
            shape(*directions.shape, dtype=BF16),
        ],
    )(
        phase.reshape(1, width),
        amplitude.reshape(1, width),
        labels.reshape(1, ROWS),
        doc_weight.reshape(1, ROWS),
        directions,
    )
    dirs[0] = copied
    dirs, docs, waves, facts, prox = lax.optimization_barrier((dirs, docs, waves, facts, prox))
    dirs_other = [across(d) for d in dirs]
    docs = docs.reshape(-1, ROWS)
    all_dirs = dirs + dirs_other
    high, low, inv_h, inv_l, send = call(
        own_kernel,
        [
            shape(ROWS, width, dtype=BF16),
            shape(ROWS, width, dtype=BF16),
            shape(ROWS, ROWS, dtype=BF16),
            shape(ROWS, ROWS, dtype=BF16),
            shape(C + 8, ROWS),
        ],
    )(docs, waves, prox, *all_dirs)

    docs_z, _ = lax.optimization_barrier((gather_line(docs, along_z), send))
    quarter = [shape(4 * ROWS, width, dtype=BF16), shape(4 * ROWS, width, dtype=BF16)]
    near_h, near_l = call(
        near_kernel, quarter, [pltpu.VMEM((3 * ROWS, docs.shape[0]), BF16)], flops=10**7
    )(*docs_z[1:], high, low, waves, *all_dirs)

    state = [prox]
    for k in range(1, ITERS + 1):
        last = k == ITERS
        parts = 1 if k == 1 else 2
        if last:
            outs = [shape(ROWS, C), shape(width, C)]
            mats = []
        else:
            outs = [
                shape(C, width),
                shape(C, width),
                shape(C, width),
                shape(7 * C + 8, ROWS),
                shape(2 * C + 8, ROWS),
            ]
            mats = [near_h, near_l, inv_h, inv_l]
        zs = gather_line(send, along_z)
        ys = gather_line(send, along_y)
        if k == 1:
            zs, ys, near_h, near_l = lax.optimization_barrier((zs, ys, near_h, near_l))
        else:
            ys = lax.optimization_barrier(ys)
        line = (ys[0] + ys[1]) + (ys[2] + ys[3])
        if k > 1:
            zs, _ = lax.optimization_barrier((zs, line))
        xs = gather_line(line, along_x)
        if k == 1:
            docs_z, _ = lax.optimization_barrier((docs_z, line))
            far_h, far_l = call(
                far_kernel, quarter, [pltpu.VMEM((4 * ROWS, docs.shape[0]), BF16)], flops=10**10
            )(across(jnp.stack(docs_z)), waves, *all_dirs)
        spread = call(
            functools.partial(spread_kernel, parts),
            [shape(C + 8, width), shape(C, width)][:parts],
            [pltpu.VMEM((2 * parts * C, ND * ROWS), BF16)],
        )(*zs, across(jnp.stack(zs)), near_h, near_l, far_h, far_l)
        out = call(functools.partial(step_kernel, k, last), outs)(
            *xs, send, facts, *spread, *mats, *state
        )
        if not last:
            *state, send = out
    return tuple(out)


def solution(mesh):
    in_specs = (P("doc", "feat"), P("doc", "feat"), P("feat"), P("feat"), P("doc"), P("doc"))
    out_specs = (P("doc", None), P("feat", None))
    return jax.shard_map(
        per_device, mesh=mesh, in_specs=in_specs, out_specs=out_specs, check_vma=False
    )
```

```python
import functools

import jax
import jax.numpy as jnp
from jax import lax
from jax.experimental import pallas as pl
from jax.experimental.pallas import tpu as pltpu
from jax.sharding import PartitionSpec as P

C = 128
ITERS = 3
NEWTON = 3
ND = 8
NF = 16
ROWS = 128
CHUNK = 256

shrink_level = 0.1
ratio_floor = 1e-06

AXES = ("doc", "feat")
F32 = jnp.float32
BF16 = jnp.bfloat16
SIN_TERMS = (
    0.07765547442052619,
    -0.5982903290573769,
    2.5500773950715985,
    -5.1677100781672785,
    3.1415926400973193,
)
INV_TWO_PI = 0.15915494309189535


def nn(a, b):
    return lax.dot_general(a, b, (((1,), (0,)), ((), ())), preferred_element_type=F32)


def nt(a, b):
    return lax.dot_general(a, b, (((1,), (1,)), ((), ())), preferred_element_type=F32)


def split(v):
    high = v.astype(BF16)
    return high, (v - high.astype(F32)).astype(BF16)


def product(a, b, dot=nn):
    ah, al = split(a)
    bh, bl = split(b)
    return dot(ah, bh) + (dot(ah, bl) + dot(al, bh))


def split3(v):
    high = v.astype(BF16)
    rest = v - high.astype(F32)
    mid = rest.astype(BF16)
    return high, mid, (rest - mid.astype(F32)).astype(BF16)


def full_product(a, b):
    ah, am, al = split3(a)
    bh, bm, bl = split3(b)
    small = nn(am, bm) + (nn(ah, bl) + nn(al, bh))
    return nn(ah, bh) + ((nn(ah, bm) + nn(am, bh)) + small)


def feature_values(dots, waves, cols):
    turns = dots * INV_TWO_PI + waves[0:1, cols]
    part = turns - jnp.round(turns)
    square = part * part
    series = SIN_TERMS[0]
    for term in SIN_TERMS[1:]:
        series = series * square + term
    sine = series * part
    return split(waves[1:2, cols] - waves[2:3, cols] * (sine * sine))


def logistic_prox(target, signs, weight_ratio):
    current = target
    for _ in range(NEWTON):
        chance = 1.0 / (1.0 + jnp.exp(signs * current))
        gradient = current - target - weight_ratio * signs * chance
        current = current - gradient / (1.0 + weight_ratio * chance * (1.0 - chance))
    return current


def signs_of(labels_ref):
    labels = labels_ref[...]
    classes = lax.broadcasted_iota(jnp.int32, (C, ROWS), 0)
    return jnp.where(jnp.broadcast_to(labels, (C, ROWS)) == classes, 1.0, -1.0).astype(F32)


def total(v):
    return jnp.sum(jnp.sum(v, axis=0, keepdims=True), axis=1, keepdims=True)


def pack(values):
    lane = lax.broadcasted_iota(jnp.int32, (8, 128), 1)
    out = jnp.zeros((8, 128), F32)
    for k, v in enumerate(values):
        if v is not None:
            out = jnp.where(lane == k, jnp.broadcast_to(v, (8, 128)), out)
    return out


def inverse(matrix):
    n = matrix.shape[0]
    row_id = lax.broadcasted_iota(jnp.int32, (n, n), 0)
    col_id = lax.broadcasted_iota(jnp.int32, (n, n), 1)
    unit = jnp.where(row_id == col_id, 1.0, 0.0)
    top = jnp.max(jnp.sum(jnp.abs(matrix), axis=0))
    alpha = 2.0 / (top + 1.0)
    residual = unit - matrix * alpha
    guess = unit * alpha
    shrink = (top - 1.0) * (0.5 * alpha)

    def wide(carry):
        return carry[2] > 1e-4

    def double(carry):
        x, r, rate = carry
        rh, rl = split(r)
        xh, xl = split(x)
        both = nn(jnp.concatenate([xh, rh, xl, rl], axis=0), rh)
        cross = nn(jnp.concatenate([xh, rh], axis=0), rl)
        both = both[: 2 * n] + (both[2 * n :] + cross)
        return x + both[:n], both[n:], rate * rate

    guess, _, _ = lax.while_loop(wide, double, (guess, residual, shrink))

    def inexact(carry):
        return jnp.logical_and(carry[1] > 1e-3, carry[2] < 6)

    def correct(carry):
        x, _, count = carry
        r = unit - full_product(matrix, x)
        size = jnp.max(jnp.sum(jnp.abs(r), axis=0))
        return x + product(x, r), size, count + 1

    start = (guess, jnp.float32(1.0), jnp.int32(0))
    guess, _, _ = lax.while_loop(inexact, correct, start)
    return guess


def doc_piece(docs_ref, slot):
    place = lax.axis_index("doc")
    block = ((place // 2 - slot // 2 + 4) % 4) * 2 + (place % 2 + slot % 2) % 2
    feat = lax.axis_index("feat")
    rows = docs_ref.shape[0] // NF
    pieces = []
    for half in range(2):
        source = 2 * block + half
        spot = source
        pieces.append(docs_ref[pl.ds(pl.multiple_of(rows * spot, rows), rows), :])
    return jnp.concatenate(pieces, axis=0)


def prepare_kernel(phase, amp, labels, weight, dirs, waves, facts, prox_ref, copied):
    copied[...] = dirs[...]
    width = phase.shape[1]
    scale = amp[...] * (2.0 / width) ** 0.5
    waves[0:1, :] = phase[...] * INV_TWO_PI
    waves[1:2, :] = scale
    waves[2:3, :] = scale + scale
    signs = signs_of(labels)
    wide = jnp.broadcast_to(weight[...], (C, ROWS))
    facts[0:C, :] = signs
    facts[C : 2 * C, :] = wide
    prox_ref[...] = logistic_prox(jnp.zeros((C, ROWS), F32), signs, wide)


def own_kernel(docs, waves, prox, d0, d1, d2, d3, e0, e1, e2, e3, high, low, inv_h, inv_l, send):
    dirs = (d0, e0, d1, e1, d2, e2, d3, e3)
    left = jnp.concatenate([doc_piece(docs, s) for s in range(ND)], axis=0)
    left = left.astype(F32).T.astype(BF16)
    width = waves.shape[1]
    gram = jnp.zeros((ROWS, 2 * ROWS), F32)
    for start in range(0, width, CHUNK):
        cols = pl.ds(start, CHUNK)
        right = jnp.concatenate([d[:, cols] for d in dirs], axis=0)
        vh, vl = feature_values(nn(left, right), waves, cols)
        high[:, cols] = vh
        low[:, cols] = vl
        gram = gram + nt(vh, jnp.concatenate([vh, vl], axis=0))
    cross = gram[:, ROWS:]
    row_id = lax.broadcasted_iota(jnp.int32, (ROWS, ROWS), 0)
    col_id = lax.broadcasted_iota(jnp.int32, (ROWS, ROWS), 1)
    whole = gram[:, :ROWS] + (cross + cross.T) + jnp.where(row_id == col_id, 1.0, 0.0)
    inv = inverse(whole)
    ih, il = split(inv)
    inv_h[...] = ih
    inv_l[...] = il
    right_side = prox[...] * (1.0 / NF)
    w = product(right_side, inv)
    send[0:C, :] = w
    send[C : C + 8, :] = pack([None, None, total(w * (right_side - w))])


def fill_blocks(left_ref, blocks, dirs, waves, high, low, first):
    width = waves.shape[1]
    for b, block in enumerate(blocks):
        left = jnp.concatenate([doc_piece(block, s) for s in range(ND)], axis=0)
        left_ref[b * ROWS : (b + 1) * ROWS, :] = left.astype(F32).T.astype(BF16)

    def step(c, carry):
        cols = pl.ds(pl.multiple_of(c * CHUNK, CHUNK), CHUNK)
        right = jnp.concatenate([d[:, cols] for d in dirs], axis=0)
        for b in range(len(blocks)):
            dots = nn(left_ref[b * ROWS : (b + 1) * ROWS, :], right)
            vh, vl = feature_values(dots, waves, cols)
            high[(first + b) * ROWS : (first + b + 1) * ROWS, cols] = vh
            low[(first + b) * ROWS : (first + b + 1) * ROWS, cols] = vl
        return carry

    lax.fori_loop(0, width // CHUNK, step, 0, unroll=4)


def near_kernel(docs_1, docs_2, docs_3, own_h, own_l, waves, d0, d1, d2, d3, e0, e1, e2, e3, high, low, left_ref):
    high[0:ROWS, :] = own_h[...]
    low[0:ROWS, :] = own_l[...]
    dirs = (d0, e0, d1, e1, d2, e2, d3, e3)
    fill_blocks(left_ref, [docs_1, docs_2, docs_3], dirs, waves, high, low, 1)


def far_kernel(docs, waves, d0, d1, d2, d3, e0, e1, e2, e3, high, low, left_ref):
    dirs = (d0, e0, d1, e1, d2, e2, d3, e3)
    fill_blocks(left_ref, [docs.at[b] for b in range(4)], dirs, waves, high, low, 0)


def spread_kernel(parts, *refs):
    near, refs = refs[:4], refs[4:]
    far, mats, refs = refs[0], refs[1:5], refs[5:]
    outs, wide = refs[:parts], refs[parts]
    width = mats[0].shape[1]
    n_rows = near[0].shape[0]
    blocks = list(near) + [far.at[b] for b in range(4)]
    tail = jnp.zeros((8, ROWS), F32)
    for slot, ref in enumerate(blocks):
        cols = pl.ds(slot * ROWS, ROWS)
        tail = tail + ref[n_rows - 8 : n_rows, :]
        for part in range(parts):
            qh, ql = split(ref[part * C : (part + 1) * C, :])
            wide[part * C : (part + 1) * C, cols] = qh
            wide[(parts + part) * C : (parts + part + 1) * C, cols] = ql
    outs[0][C : C + 8, 0:ROWS] = tail
    count = parts * C
    depth = 4 * ROWS

    def chunk(c, carry):
        cols = pl.ds(pl.multiple_of(c * CHUNK, CHUNK), CHUNK)
        both = nn(wide[:, :depth], mats[0][:, cols]) + nn(wide[:, depth:], mats[2][:, cols])
        cross = nn(wide[:count, :depth], mats[1][:, cols]) + nn(wide[:count, depth:], mats[3][:, cols])
        result = both[:count] + (both[count:] + cross)
        for part in range(parts):
            outs[part][0:C, cols] = result[part * C : (part + 1) * C]
        return carry

    lax.fori_loop(0, width // CHUNK, chunk, 0, unroll=True)


def step_kernel(k, last, *refs):
    it = iter(refs)
    take = lambda n: [next(it) for _ in range(n)]
    feat_in = take(4)
    own, facts = take(2)
    spread = take(1 if k == 1 else 2)
    if not last:
        oh, ol, inv_h, inv_l = take(4)
    if k == 1:
        prox_prev, = take(1)
    else:
        z_prev, v_prev, e_prev, small = take(4)
    if last:
        out_m, out_z = take(2)
    else:
        z_out, v_out, e_out, small_out, send = take(5)
    width = spread[0].shape[1]
    n_rows = own.shape[0]

    def feat_total(rows):
        return (feat_in[0][rows, :] + feat_in[1][rows, :]) + (feat_in[2][rows, :] + feat_in[3][rows, :])

    feat_scalars = feat_total(pl.ds(n_rows - 8, 8))[0:1, :]
    doc_scalars = spread[0][C : C + 1, 0:ROWS]
    first = pl.ds(0, C)
    second = pl.ds(C, C)
    at = lambda row, n: row[:, n : n + 1]
    if k == 1:
        rho = jnp.ones((1, 1), F32)
        inv_g = None
        quad = at(doc_scalars, 2)
    else:
        rho_prev = small[7 * C : 7 * C + 1, 0:1]
        primal = at(feat_scalars, 0) + at(doc_scalars, 5)
        dual = rho_prev * rho_prev * (ND * at(feat_scalars, 1) + at(doc_scalars, 6))
        g = jnp.sqrt(jnp.sqrt((primal + ratio_floor) / (dual + ratio_floor)))
        rho = rho_prev * g
        inv_g = 1.0 / g
        quad = at(doc_scalars, 2) + inv_g * (at(doc_scalars, 3) + inv_g * at(doc_scalars, 4))

    limit = shrink_level / (rho * ND)

    def chunk(c, carry):
        az, norm_p, norm_d = carry
        cols = pl.ds(pl.multiple_of(c * CHUNK, CHUNK), CHUNK)
        if k == 1:
            v = qsum = spread[0][0:C, cols]
            target = v * (1.0 / ND)
            z = target - jnp.clip(target, -limit, limit)
            e = -z
            p = e
        else:
            qsum = spread[0][0:C, cols] + spread[1][0:C, cols] * inv_g
            v = qsum + v_prev[:, cols] * inv_g
            z_old = z_prev[:, cols]
            target = z_old + v * (1.0 / ND)
            z = target - jnp.clip(target, -limit, limit)
            e = z_old - z
            p = e - e_prev[:, cols] * inv_g
        if last:
            out_z[cols, :] = (z * float(NF)).T
            return carry
        v_out[:, cols] = v
        z_out[:, cols] = z
        e_out[:, cols] = e
        norm_p = norm_p + jnp.sum(p * (ND * p + 2.0 * qsum), axis=0, keepdims=True)
        norm_d = norm_d + jnp.sum(e * e, axis=0, keepdims=True)
        zh, zl = split(z)
        az2 = nt(jnp.concatenate([zh, zl], axis=0), oh[0:ROWS, cols])
        az = az + ((az2[:C] + az2[C:]) + nt(zh, ol[0:ROWS, cols]))
        return az, norm_p, norm_d

    init = (jnp.zeros((C, ROWS), F32), jnp.zeros((1, CHUNK), F32), jnp.zeros((1, CHUNK), F32))
    az, norm_p, norm_d = lax.fori_loop(0, width // CHUNK, chunk, init, unroll=True)

    signs = facts[0:C, :]
    ratio = facts[C : 2 * C, :] / rho
    w_sum = feat_total(first)
    if k == 1:
        m_prev = prox_prev[...]
    else:
        m_prev = small[0:C, :]
        w_sum = w_sum + (feat_total(second) + small[C : 2 * C, :]) * inv_g
    target = m_prev - w_sum
    margins = logistic_prox(target, signs, ratio)
    if last:
        out_m[...] = margins.T
        return
    if k == 1:
        b_prev = jnp.zeros((C, ROWS), F32)
        w = own[first, :]
        y = m_prev * (1.0 / NF) - w
        az_prev = jnp.zeros((C, ROWS), F32)
    else:
        b_prev = small[2 * C : 3 * C, :] * inv_g
        w = own[first, :] + (own[second, :] + small[3 * C : 4 * C, :]) * inv_g
        y = small[4 * C : 5 * C, :] + (m_prev - b_prev - small[5 * C : 6 * C, :]) * (1.0 / NF) - w
        az_prev = small[6 * C : 7 * C, :]
    b_new = target - margins
    sums = target - b_prev
    small_out[0:C, :] = margins
    small_out[C : 2 * C, :] = w_sum
    small_out[2 * C : 3 * C, :] = b_new
    small_out[3 * C : 4 * C, :] = w
    small_out[4 * C : 5 * C, :] = y
    small_out[5 * C : 6 * C, :] = sums
    small_out[6 * C : 7 * C, :] = az
    small_out[7 * C : 7 * C + 8, :] = jnp.broadcast_to(rho, (8, 128))
    ru = y + (margins - sums) * (1.0 / NF) - az
    rv = az_prev - az - w - b_new * (1.0 / NF)
    rh, rl = split(jnp.concatenate([ru, rv], axis=0))
    ih = inv_h[...]
    solved = nn(rh, ih) + (nn(rl, ih) + nn(rh, inv_l[...]))
    u = solved[:C]
    v2 = solved[C:]
    send[0:C, :] = u
    send[C : 2 * C, :] = v2
    part = rv - v2
    gap = sums - margins
    move = margins - m_prev
    send[2 * C : 2 * C + 8, :] = pack(
        [
            jnp.sum(norm_p, axis=1, keepdims=True) + quad,
            jnp.sum(norm_d, axis=1, keepdims=True),
            total(u * (ru - u)),
            2.0 * total(u * part),
            total(v2 * part),
            total(gap * gap),
            total(move * move),
        ]
    )


def table(move):
    pairs = []
    for d in range(ND):
        for f in range(NF):
            z, core, x, y = d // 2, d % 2, f // 4, f % 4
            z2, core2, x2, y2 = move(z, core, x, y)
            pairs.append((d * NF + f, ((z2 % 4) * 2 + core2) * NF + (x2 % 4) * 4 + y2 % 4))
    return pairs


def along_y(v, k):
    return lax.ppermute(v, AXES, table(lambda z, c, x, y: (z, c, x, y + k)))


def along_x(v, k):
    return lax.ppermute(v, AXES, table(lambda z, c, x, y: (z, c, x + k, y)))


def along_z(v, k):
    return lax.ppermute(v, AXES, table(lambda z, c, x, y: (z + k, c, x, y)))


def across(v):
    return lax.ppermute(v, AXES, table(lambda z, c, x, y: (z, 1 - c, x, y)))


def call(body, outs, scratch=(), flops=0, limit=24):
    return pl.pallas_call(
        body,
        out_shape=outs,
        scratch_shapes=list(scratch),
        cost_estimate=pl.CostEstimate(flops=flops, bytes_accessed=0, transcendentals=0),
        compiler_params=pltpu.CompilerParams(vmem_limit_bytes=limit * 1024 * 1024),
    )


def shape(*dims, dtype=F32):
    return jax.ShapeDtypeStruct(dims, dtype)


def gather_line(v, move):
    return [v] + [move(v, k) for k in (1, 2, 3)]


def per_device(documents, directions, phase, amplitude, doc_weight, labels):
    width = directions.shape[1]
    dirs = gather_line(directions, along_z)
    docs = lax.all_to_all(
        jnp.broadcast_to(documents.T[None], (NF,) + documents.T.shape), "feat", 0, 0
    )
    waves, facts, prox, copied = call(
        prepare_kernel,
        [
            shape(8, width),
            shape(2 * C, ROWS),
            shape(C, ROWS),
            shape(*directions.shape, dtype=BF16),
        ],
    )(
        phase.reshape(1, width),
        amplitude.reshape(1, width),
        labels.reshape(1, ROWS),
        doc_weight.reshape(1, ROWS),
        directions,
    )
    dirs[0] = copied
    dirs, docs, waves, facts, prox = lax.optimization_barrier((dirs, docs, waves, facts, prox))
    dirs_other = [across(d) for d in dirs]
    docs = docs.reshape(-1, ROWS)
    all_dirs = dirs + dirs_other
    high, low, inv_h, inv_l, send = call(
        own_kernel,
        [
            shape(ROWS, width, dtype=BF16),
            shape(ROWS, width, dtype=BF16),
            shape(ROWS, ROWS, dtype=BF16),
            shape(ROWS, ROWS, dtype=BF16),
            shape(C + 8, ROWS),
        ],
    )(docs, waves, prox, *all_dirs)

    docs_z, _ = lax.optimization_barrier((gather_line(docs, along_z), send))
    quarter = [shape(4 * ROWS, width, dtype=BF16), shape(4 * ROWS, width, dtype=BF16)]
    near_h, near_l = call(
        near_kernel, quarter, [pltpu.VMEM((3 * ROWS, docs.shape[0]), BF16)], flops=10**7
    )(*docs_z[1:], high, low, waves, *all_dirs)

    state = [prox]
    for k in range(1, ITERS + 1):
        last = k == ITERS
        parts = 1 if k == 1 else 2
        if last:
            outs = [shape(ROWS, C), shape(width, C)]
            mats = []
        else:
            outs = [
                shape(C, width),
                shape(C, width),
                shape(C, width),
                shape(7 * C + 8, ROWS),
                shape(2 * C + 8, ROWS),
            ]
            mats = [near_h, near_l, inv_h, inv_l]
        zs = gather_line(send, along_z)
        ys = gather_line(send, along_y)
        if k == 1:
            zs, ys, near_h, near_l = lax.optimization_barrier((zs, ys, near_h, near_l))
        else:
            ys = lax.optimization_barrier(ys)
        line = (ys[0] + ys[1]) + (ys[2] + ys[3])
        if k > 1:
            zs, _ = lax.optimization_barrier((zs, line))
        xs = gather_line(line, along_x)
        if k == 1:
            docs_z, _ = lax.optimization_barrier((docs_z, line))
            far_h, far_l = call(
                far_kernel, quarter, [pltpu.VMEM((4 * ROWS, docs.shape[0]), BF16)], flops=10**10
            )(across(jnp.stack(docs_z)), waves, *all_dirs)
        spread = call(
            functools.partial(spread_kernel, parts),
            [shape(C + 8, width), shape(C, width)][:parts],
            [pltpu.VMEM((2 * parts * C, ND * ROWS), BF16)],
        )(*zs, across(jnp.stack(zs)), near_h, near_l, far_h, far_l)
        out = call(functools.partial(step_kernel, k, last), outs)(
            *xs, send, facts, *spread, *mats, *state
        )
        if not last:
            *state, send = out
    return tuple(out)


def solution(mesh):
    in_specs = (P("doc", "feat"), P("doc", "feat"), P("feat"), P("feat"), P("doc"), P("doc"))
    out_specs = (P("doc", None), P("feat", None))
    return jax.shard_map(
        per_device, mesh=mesh, in_specs=in_specs, out_specs=out_specs, check_vma=False
    )
```
